1024 devices in a mesh: pair: 128 (over y, z), slab: 8 (over x, core).
Axes of the slice: x: 4, y: 4, z: 32, core: 2. Of those that a mesh axis runs over, the one named last changes fastest.
Arguments:
- amplitudes: bfloat16 [3072, 8, 2048], P(None, 'slab', 'pair'), may hold values from -6 to 6
- ladder_integral: bfloat16 [16384, 16384], P('slab', 'pair'), may hold values from -0.046875 to 0.046875
- tile_mask: int32 [128, 128], P('slab', 'pair'), may hold values 0 or 1
- left_factor: bfloat16 [128, 384, 4096], P(None, 'pair', 'slab'), may hold values from -0.0048828125 to 0.0048828125
- right_factor: float32 [128, 4096, 384], P(None, 'pair'), may hold values from -0.5 to 0.5
Outputs:
- residual: float32 [3072, 16384], P('slab', 'pair')
The draws below stay inside these ranges and needn't reach their ends.
Inputs may be any that keep to these rules, and one draw needn't show every extreme that they name: `tile_mask`: 1 where a pair of tiles may couple, else 0.
All inputs are finite; a program needn't handle non-finite values. No bound on the sum of `tile_mask` on one device may be relied on, other than what follows from the above.
Results may differ from the reference program's by a relative error of at most 0.0003.
Values may be sent and summed in bfloat16 or wider, within the bound.
A program may use at most 64 MiB of HBM per device.

```python
import jax
import jax.numpy as jnp
from jax import lax

O = 384
V = 4096
TILE = 128
NA = 4
NI = 8
L = 128
ROWS = 3072
NP = 16384
NT = 128
N_SLAB = 8


def set_ends(array, own_key, low, high):
    place = [jax.random.randint(jax.random.fold_in(own_key, axis), (), 0, length) for axis, length in enumerate(array.shape)]
    widest = array.shape.index(max(array.shape))
    neighbour = place[:widest] + [(place[widest] + 1) % array.shape[widest]] + place[widest + 1:]
    return array.at[tuple(place)].set(low).at[tuple(neighbour)].set(high)


def steps_of(rng, shape, cuts, least, largest):
    def one(position, parts):
        steps = jax.random.uniform(jax.random.fold_in(jax.random.fold_in(rng, 6), position), (parts,), jnp.float32, least / len(cuts), largest / len(cuts))
        return jnp.repeat(jnp.exp(steps), shape[position] // parts).reshape((-1,) + (1,) * (len(shape) - position - 1))

    gain = one(*cuts[0])
    for cut in cuts[1:]:
        gain = gain * one(*cut)
    return gain


def scatter_about(key, extent, scale, reach, pieces=(), kind=jnp.bfloat16):
    drawn = jax.random.normal(key, extent, jnp.float32) * scale
    if len(pieces) > 0:
        drawn = steps_of(key, extent, pieces, -0.22, 0.18) * drawn
    return jnp.clip(drawn, min=-reach, max=reach).astype(kind)


def setup_inputs(seed: int = 0) -> dict:
    splits = jax.random.split(jax.random.key(seed), 6)
    return {
        "amplitudes": scatter_about(splits[0], (ROWS, N_SLAB, NP // N_SLAB), 1.0, 6.0, ((1, 8), (2, 128))),
        "ladder_integral": scatter_about(splits[1], (NP, NP), NP ** -0.5, 0.046875, ((0, 8), (1, 128))),
        "tile_mask": set_ends((jax.random.randint(splits[2], (NT, NT), 0, 4) < 3).astype(jnp.int32), jax.random.fold_in(splits[2], 1), 0, 1),
        "left_factor": scatter_about(splits[3], (L, O, V), (O * V) ** -0.5, 0.0048828125, ((1, 128), (2, 8))),
        "right_factor": scatter_about(splits[4], (L, V, O), L ** -0.5, 0.5, ((1, 128),), jnp.float32),
    }


def reference(amplitudes, ladder_integral, tile_mask, left_factor, right_factor):
    row_count = NI * O
    pair_total = NA * V
    flat_amps = amplitudes.reshape(row_count, pair_total)
    wide_amps = flat_amps.astype(jnp.float32)
    tile_cols = pair_total // TILE // 8

    def ladder_block(block_index):
        weights = lax.dynamic_slice_in_dim(ladder_integral, block_index * tile_cols * TILE, tile_cols * TILE, 1)
        pattern = lax.dynamic_slice_in_dim(tile_mask, block_index * tile_cols, tile_cols, 1)
        spread = jnp.repeat(jnp.repeat(pattern, TILE, axis=0), TILE, axis=1).astype(jnp.bfloat16)
        masked = (weights * spread).astype(jnp.float32)
        return jnp.dot(wide_amps, masked, precision=lax.Precision.HIGHEST)

    blocks = lax.map(ladder_block, jnp.arange(8, dtype=jnp.int32))
    ladder = jnp.transpose(blocks, (1, 0, 2)).reshape(row_count, pair_total)
    amps_four = wide_amps.reshape(NI, O, V, NA)
    cycle_mix = jnp.einsum("ikca,lkc->ial", amps_four, left_factor.astype(jnp.float32), precision=lax.Precision.HIGHEST)
    cycle = jnp.einsum("ial,lbj->ijba", cycle_mix, right_factor.astype(jnp.float32), precision=lax.Precision.HIGHEST)
    return ladder + cycle.reshape(row_count, pair_total)
```

```python
import jax
import jax.numpy as jnp
from jax import lax
from jax.experimental import pallas as pl
from jax.experimental.pallas import tpu as pltpu
from jax.sharding import PartitionSpec as P

O = 384
NA = 4
NI = 8
NY = 4
NZ = 32
NX = 4
NS = 8
KQ = O // NY // 2
HR = NI * KQ
MESH = pl.DeviceIdType.MESH
F32 = jnp.float32
BF16 = jnp.bfloat16
Z_PHASES = ((1, 3), (4, 3), (16, 1))
Z_SHIFTS = tuple(w * q for w, n in Z_PHASES for q in range(1, n + 1))
DOT0 = (((0,), (0,)), ((), ()))


def kernel(
    t_ref, int_ref, mask_ref, left_ref, lad_ref, mix_ref,
    tg, ig, acc, sib, xin, red, fin, tsel, mixp, mslab, mone, myin, mzsend, mzin,
    ys_send, ys_recv, ig_send, ig_recv, z_send, z_recv, sib_sem, x_send, x_recv, yo_send, yo_recv,
    ms_send, ms_recv, my_send, my_recv, mz_send, mz_recv,
):
    pair = lax.axis_index("pair")
    slab = lax.axis_index("slab")
    y, z = lax.div(pair, NZ), lax.rem(pair, NZ)
    x, c = lax.div(slab, 2), lax.rem(slab, 2)

    def at_y(q):
        return {"pair": lax.rem(y + q, NY) * NZ + z, "slab": slab}

    def at_z(q):
        return {"pair": y * NZ + lax.rem(z + q + NZ, NZ), "slab": slab}

    def at_slab(q):
        return {"pair": pair, "slab": lax.rem(slab + q, NS)}

    def at_x(q):
        return {"pair": pair, "slab": lax.rem(x + q, NX) * 2 + c}

    sibling = {"pair": pair, "slab": slab + 1 - 2 * c}

    def remote(src, dst, send, recv, where):
        return pltpu.make_async_remote_copy(
            src_ref=src, dst_ref=dst, send_sem=send, recv_sem=recv, device_id=where, device_id_type=MESH
        )

    barrier = pltpu.get_barrier_semaphore()
    senders = [at_y(q) for q in range(1, NY)] + [at_z(1)] + [at_z(-q) for q in Z_SHIFTS]
    senders += [at_slab(q) for q in range(1, NS)]
    for where in senders:
        pl.semaphore_signal(barrier, inc=1, device_id=where, device_id_type=MESH)

    for tile in range(16):
        rows = int_ref[tile // 4, (tile % 4) * 8:(tile % 4) * 8 + 8]
        keep = mask_ref[tile].astype(F32)
        ig[tile // 4, (tile % 4) * 8:(tile % 4) * 8 + 8, :, 0:128] = (rows.astype(F32) * keep).astype(BF16)
    acc[...] = jnp.zeros_like(acc)
    mixp[...] = jnp.zeros_like(mixp)

    pl.semaphore_wait(barrier, len(senders))

    def y_copy(q):
        return remote(t_ref.at[lax.rem(y + q, NY)], tg.at[:, y, z], ys_send.at[q - 1], ys_recv.at[q - 1], at_y(q))

    def y_arrived(q):
        return remote(t_ref.at[0], tg.at[:, lax.rem(y + NY - q, NY), z], ys_send.at[q - 1], ys_recv.at[q - 1], at_y(q))

    for q in range(1, NY):
        y_copy(q).start()
    tg[:, y, z] = t_ref[y]

    def ig_copy(n, where):
        slot_src, slot_dst, first, count = ((0, 3, 0, 4), (0, 1, 0, 4), (3, 2, 0, 2), (1, 2, 2, 2))[n]
        return remote(
            ig.at[first:first + count, :, :, slot_src * 128:slot_src * 128 + 128],
            ig.at[first:first + count, :, :, slot_dst * 128:slot_dst * 128 + 128],
            ig_send.at[n], ig_recv.at[n], where,
        )

    ig_copies = [ig_copy(n, at_y(1 if n % 2 == 0 else NY - 1)) for n in range(4)]
    ig_copies[0].start()
    ig_copies[1].start()

    for q in range(1, NY):
        y_arrived(q).wait_recv()

    def z_copy(way, h, step):
        sign = 1 - 2 * way
        slot = lax.rem(z - sign * (step - 1) + NZ, NZ)
        return remote(
            tg.at[h, :, slot], tg.at[h, :, slot], z_send.at[way, h, step], z_recv.at[way, h, step], at_z(sign)
        )

    def z_arrived(way, h, step):
        sign = 1 - 2 * way
        slot = lax.rem(z - sign * step + NZ, NZ)
        return remote(
            tg.at[h, :, slot], tg.at[h, :, slot], z_send.at[way, h, step], z_recv.at[way, h, step], at_z(sign)
        )

    streams = [(way, h) for h in range(2) for way in range(2)]
    for way, h in streams:
        z_copy(way, h, 1).start()

    def forward(step):
        for way, h in streams:
            z_arrived(way, h, step).wait_recv()
            z_copy(way, h, step + 1).start()

    def multiply(first, second):
        rhs = jnp.concatenate([ig[:, first].reshape(64, 512), ig[:, second].reshape(64, 512)], axis=0)
        for h in range(2):
            lhs = jnp.concatenate([tg[h, :, first].reshape(64, HR), tg[h, :, second].reshape(64, HR)], axis=0)
            acc[h] += lax.dot_general(lhs, rhs, DOT0, preferred_element_type=F32).reshape(NX, 2, KQ, 512)

    def unit(distance):
        multiply(lax.rem(z + NZ - distance, NZ), lax.rem(z + distance, NZ))

    @pl.loop(1, 4)
    def _(step):
        forward(step)

    ig_copies[0].wait_recv()
    ig_copies[2].start()
    ig_copies[1].wait_recv()
    ig_copies[3].start()

    @pl.loop(4, 8)
    def _(step):
        forward(step)

    ig_copies[2].wait_recv()
    ig_copies[3].wait_recv()

    @pl.loop(8, 15)
    def _(step):
        forward(step)
        unit(2 * step - 15)
        unit(2 * step - 14)

    for way, h in streams:
        z_arrived(way, h, 15).wait_recv()
    z_copy(0, 0, 16).start()
    z_copy(1, 1, 16).start()
    unit(15)
    z_arrived(0, 0, 16).wait_recv()
    z_arrived(1, 1, 16).wait_recv()
    multiply(z, lax.rem(z + 16, NZ))

    sib_copy = remote(acc.at[:, :, 1 - c], sib, sib_sem.at[0], sib_sem.at[1], sibling)
    sib_copy.start()

    lane = lax.broadcasted_iota(jnp.int32, (HR, 128), 1)
    row = lax.broadcasted_iota(jnp.int32, (HR, 128), 0)
    for h in range(2):
        k_own = 3 * z + (lane >> 3) - KQ * h
        hit = (row == KQ * (lane & 7) + k_own) & (k_own >= 0) & (k_own < KQ) & (lane < 24)
        pick = jnp.where(hit, 1.0, 0.0).astype(BF16)
        got = jnp.dot(tg[h].reshape(2048, HR), pick, preferred_element_type=F32)
        if h == 0:
            tsel[...] = got
        else:
            tsel[...] += got
    for a in range(NA):
        own = tsel[pl.ds(a, 512, stride=NA), :].astype(BF16)
        part = jnp.zeros((8, 128), F32)
        for d in range(3):
            whole = lax.dot_general(own, left_ref[d], (((0,), (1,)), ((), ())), preferred_element_type=F32)
            part += whole[8 * d:8 * d + 8]
        mixp[:, a] = part

    def ms_copy(q):
        return remote(mixp.at[lax.rem(slab + q, NS)], mslab.at[q - 1], ms_send.at[q - 1], ms_recv.at[q - 1], at_slab(q))

    for q in range(1, NS):
        ms_copy(q).start()

    sib_copy.wait()

    def x_copy(q):
        return remote(acc.at[:, lax.rem(x + q, NX), c], xin.at[q - 1], x_send.at[q - 1], x_recv.at[q - 1], at_x(q))

    for q in (2, 1, 3):
        there = lax.rem(x + q, NX)
        acc[:, there, c] = acc[:, there, c] + sib[:, there]
        x_copy(q).start()

    for q in range(1, NS):
        ms_copy(q).wait_recv()
    total = mixp[slab]
    for q in range(1, NS):
        total += mslab[q - 1]
    mone[...] = total

    def my_copy(q):
        return remote(mone, myin.at[q - 1], my_send.at[q - 1], my_recv.at[q - 1], at_y(q))

    for q in range(1, NY):
        my_copy(q).start()
    for q in range(1, NY):
        my_copy(q).wait_recv()
        total += myin[q - 1]

    mz_copies = []
    n = 0
    for phase, (width, count) in enumerate(Z_PHASES):
        mzsend[phase] = total
        for q in range(1, count + 1):
            mz_copies.append(remote(mzsend.at[phase], mzin.at[n], mz_send.at[n], mz_recv.at[n], at_z(width * q)))
            mz_copies[n].start()
            n += 1
        if phase == 1:
            mine = acc[:, x, c] + sib[:, x]
            for q in range(1, NX):
                x_copy(q).wait_recv()
                mine += xin[q - 1]
            red[...] = mine

            def yo_copy(q):
                return remote(
                    red.at[:, :, 128 * q:128 * q + 128], fin.at[y], yo_send.at[q - 1], yo_recv.at[q - 1], at_y(q)
                )

            for q in range(1, NY):
                yo_copy(q).start()
            fin[y] = red[:, :, 0:128]
        for k in range(n - count, n):
            mz_copies[k].wait_recv()
            total += mzin[k]
    mix_ref[...] = total

    for q in range(1, NY):
        remote(
            red.at[:, :, 128 * q:128 * q + 128], fin.at[lax.rem(y + NY - q, NY)],
            yo_send.at[q - 1], yo_recv.at[q - 1], at_y(q),
        ).wait_recv()
    lad_ref[...] = fin[...]

    for q in range(1, NY):
        y_copy(q).wait_send()
        my_copy(q).wait_send()
        yo_copy(q).wait_send()
    for copy in ig_copies:
        copy.wait_send()
    for way, h in streams:
        @pl.loop(1, 16)
        def _(step):
            z_copy(way, h, step).wait_send()
    z_copy(0, 0, 16).wait_send()
    z_copy(1, 1, 16).wait_send()
    for q in range(1, NX):
        x_copy(q).wait_send()
    for q in range(1, NS):
        ms_copy(q).wait_send()
    for copy in mz_copies:
        copy.wait_send()


def per_device(amplitudes, ladder_integral, tile_mask, left_factor, right_factor):
    own = amplitudes.reshape(NI, NY, 2, KQ, 16)
    relaid = jnp.transpose(own, (1, 2, 4, 0, 3)).reshape(NY, 2, 16, HR)
    integral = ladder_integral.reshape(NY, NZ, 16, 128)
    left = jnp.transpose(left_factor, (1, 0, 2))
    vmem = pl.BlockSpec(memory_space=pltpu.VMEM)
    dma = pltpu.SemaphoreType.DMA
    n_mz = len(Z_SHIFTS)
    ladder, mix = pl.pallas_call(
        kernel,
        out_shape=(
            jax.ShapeDtypeStruct((NY, 2, KQ, 128), F32),
            jax.ShapeDtypeStruct((8, 128), F32),
        ),
        in_specs=[vmem, vmem, pl.BlockSpec(memory_space=pltpu.SMEM), vmem],
        out_specs=(vmem, vmem),
        scratch_shapes=[
            pltpu.VMEM((2, NY, NZ, 16, HR), BF16),
            pltpu.VMEM((NY, NZ, 16, 512), BF16),
            pltpu.VMEM((2, NX, 2, KQ, 512), F32),
            pltpu.VMEM((2, NX, KQ, 512), F32),
            pltpu.VMEM((NX - 1, 2, KQ, 512), F32),
            pltpu.VMEM((2, KQ, 512), F32),
            pltpu.VMEM((NY, 2, KQ, 128), F32),
            pltpu.VMEM((2048, 128), F32),
            pltpu.VMEM((NS, 8, 128), F32),
            pltpu.VMEM((NS - 1, 8, 128), F32),
            pltpu.VMEM((8, 128), F32),
            pltpu.VMEM((NY - 1, 8, 128), F32),
            pltpu.VMEM((len(Z_PHASES), 8, 128), F32),
            pltpu.VMEM((n_mz, 8, 128), F32),
            dma((NY - 1,)), dma((NY - 1,)),
            dma((4,)), dma((4,)),
            dma((2, 2, 17)), dma((2, 2, 17)),
            dma((2,)),
            dma((NX - 1,)), dma((NX - 1,)),
            dma((NY - 1,)), dma((NY - 1,)),
            dma((NS - 1,)), dma((NS - 1,)),
            dma((NY - 1,)), dma((NY - 1,)),
            dma((n_mz,)), dma((n_mz,)),
        ],
        compiler_params=pltpu.CompilerParams(
            collective_id=0, has_side_effects=True, vmem_limit_bytes=40 * 1024 * 1024
        ),
    )(relaid, integral, tile_mask.reshape(16), left)
    cycle = jnp.einsum("al,lbj->jba", mix[:NA], right_factor, precision=lax.Precision.HIGHEST)
    return ladder.reshape(O, 128) + cycle.reshape(O, 128)


def solution(mesh):
    return jax.shard_map(
        per_device,
        mesh=mesh,
        in_specs=(
            P(None, "slab", "pair"),
            P("slab", "pair"),
            P("slab", "pair"),
            P(None, "pair", "slab"),
            P(None, "pair", None),
        ),
        out_specs=P("slab", "pair"),
        check_vma=False,
    )
```

```python
import jax
import jax.numpy as jnp
from jax import lax
from jax.experimental import pallas as pl
from jax.experimental.pallas import tpu as pltpu
from jax.sharding import PartitionSpec as P

O = 384
NA = 4
NI = 8
NY = 4
NZ = 32
NX = 4
NS = 8
KQ = O // NY // 2
HR = NI * KQ
MESH = pl.DeviceIdType.MESH
F32 = jnp.float32
BF16 = jnp.bfloat16
Z_PHASES = ((-3, -2, -1, 1, 2, 3, 4), (-12, -4, 4, 12))
L_PART = 8
DOT0 = (((0,), (0,)), ((), ()))


def kernel(
    t_ref, int_hbm, mask_ref, left_hbm, right_hbm, out_ref,
    int_ref, left_ref, right_ref, tsend, tg, ig, acc, sib, xin, red, fin, tsel, mixp, mslab, mone, myin, mzsend, mzin,
    rt_hi, rt_lo, spread,
    in_sem, left_in, ys_send, ys_recv, ig_send, ig_recv, z_send, z_recv, sib_send, sib_recv, x_send, x_recv, yo_send, yo_recv,
    ms_send, ms_recv, my_send, my_recv, mz_send, mz_recv,
):
    pair = lax.axis_index("pair")
    slab = lax.axis_index("slab")
    y, z = lax.div(pair, NZ), lax.rem(pair, NZ)
    x, c = lax.div(slab, 2), lax.rem(slab, 2)

    def at_y(q):
        return {"pair": lax.rem(y + q, NY) * NZ + z, "slab": slab}

    def at_z(q):
        return {"pair": y * NZ + lax.rem(z + q + NZ, NZ), "slab": slab}

    def at_slab(q):
        return {"pair": pair, "slab": lax.rem(slab + q, NS)}

    def at_x(q):
        return {"pair": pair, "slab": lax.rem(x + q, NX) * 2 + c}

    sibling = {"pair": pair, "slab": slab + 1 - 2 * c}

    def remote(src, dst, send, recv, where):
        return pltpu.make_async_remote_copy(
            src_ref=src, dst_ref=dst, send_sem=send, recv_sem=recv, device_id=where, device_id_type=MESH
        )

    loads = [
        pltpu.make_async_copy(here, there, in_sem.at[n])
        for n, (here, there) in enumerate(((int_hbm, int_ref), (left_hbm, left_ref), (right_hbm, right_ref)))
    ]
    for load in loads:
        load.start()

    barrier = pltpu.get_barrier_semaphore()
    senders = [at_y(q) for q in range(1, NY)] + [at_slab(q) for q in range(1, NS)] + [at_z(-1)]
    for where in senders:
        pl.semaphore_signal(barrier, inc=1, device_id=where, device_id_type=MESH)

    for there in range(NY):
        for h in range(2):
            first = (2 * there + h) * KQ
            tsend[there, h] = jnp.concatenate([t_ref[:, i * O + first:i * O + first + KQ] for i in range(NI)], axis=1)

    pl.semaphore_wait(barrier, len(senders))

    def y_copy(q):
        return remote(tsend.at[lax.rem(y + q, NY)], tg.at[:, y, z], ys_send.at[q - 1], ys_recv.at[q - 1], at_y(q))

    def y_arrived(q):
        return remote(tsend.at[0], tg.at[:, lax.rem(y + NY - q, NY), z], ys_send.at[q - 1], ys_recv.at[q - 1], at_y(q))

    for q in (2, 1, 3):
        y_copy(q).start()
    pl.semaphore_signal(left_in, inc=1, device_id=at_z(1), device_id_type=MESH)
    tg[:, y, z] = tsend[y]

    loads[0].wait()
    for tile in range(16):
        rows = int_ref[tile // 4, (tile % 4) * 8:(tile % 4) * 8 + 8]
        keep = mask_ref[tile].astype(F32)
        ig[tile // 4, (tile % 4) * 8:(tile % 4) * 8 + 8, :, 0:128] = (rows.astype(F32) * keep).astype(BF16)
    acc[...] = jnp.zeros_like(acc)
    mixp[...] = jnp.zeros_like(mixp)

    def ig_copy(n, where):
        slot_src, slot_dst, first, count = ((0, 3, 0, 4), (0, 1, 0, 4), (3, 2, 0, 2), (1, 2, 2, 2))[n]
        return remote(
            ig.at[first:first + count, :, :, slot_src * 128:slot_src * 128 + 128],
            ig.at[first:first + count, :, :, slot_dst * 128:slot_dst * 128 + 128],
            ig_send.at[n], ig_recv.at[n], where,
        )

    ig_copies = [ig_copy(n, at_y(1 if n % 2 == 0 else NY - 1)) for n in range(4)]
    ig_copies[0].start()
    ig_copies[1].start()

    for q in range(1, NY):
        y_arrived(q).wait_recv()

    def z_copy(stream, step, arrived=False):
        way, h, part = stream
        sign = 1 - 2 * way
        slot = lax.rem(z - sign * (step - (0 if arrived else 1)) + NZ, NZ)
        piece = tg.at[h, 2 * part:2 * part + 2, slot]
        return remote(piece, piece, z_send.at[way, h, part, step], z_recv.at[way, h, part, step], at_z(sign))

    streams = [(way, h, part) for h in range(2) for part in range(2) for way in range(2)]
    for stream in streams:
        if stream[0] == 0:
            z_copy(stream, 1).start()
    pl.semaphore_wait(left_in, 1)
    for stream in streams:
        if stream[0] == 1:
            z_copy(stream, 1).start()

    def forward(step):
        for stream in streams:
            z_copy(stream, step, True).wait_recv()
            z_copy(stream, step + 1).start()

    def split(part):
        wide = right_ref[pl.ds(part * L_PART, L_PART)].reshape(L_PART * 32, O).T
        high = wide.astype(BF16)
        where = pl.ds(pl.multiple_of(part * L_PART * 32, L_PART * 32), L_PART * 32)
        rt_hi[:, where] = high
        rt_lo[:, where] = (wide - high.astype(F32)).astype(BF16)

    loads[1].wait()
    loads[2].wait()

    def multiply(first, second):
        rhs = jnp.concatenate([ig[:, first].reshape(64, 512), ig[:, second].reshape(64, 512)], axis=0)
        for h in range(2):
            lhs = jnp.concatenate([tg[h, :, first].reshape(64, HR), tg[h, :, second].reshape(64, HR)], axis=0)
            acc[h] += lax.dot_general(lhs, rhs, DOT0, preferred_element_type=F32).reshape(NX, 2, KQ, 512)

    def unit(distance):
        multiply(lax.rem(z + NZ - distance, NZ), lax.rem(z + distance, NZ))

    @pl.loop(1, 4)
    def _(step):
        forward(step)
        split(2 * step - 2)
        split(2 * step - 1)

    ig_copies[0].wait_recv()
    ig_copies[2].start()
    ig_copies[1].wait_recv()
    ig_copies[3].start()

    @pl.loop(4, 8)
    def _(step):
        forward(step)
        split(2 * step - 2)
        split(2 * step - 1)

    split(14)
    split(15)
    ig_copies[2].wait_recv()
    ig_copies[3].wait_recv()

    @pl.loop(8, 15)
    def _(step):
        forward(step)
        unit(2 * step - 15)
        unit(2 * step - 14)

    last = [stream for stream in streams if stream[0] == stream[1]]
    for stream in streams:
        z_copy(stream, 15, True).wait_recv()
        if stream in last:
            z_copy(stream, 16).start()
    unit(15)
    for stream in last:
        z_copy(stream, 16, True).wait_recv()
    multiply(z, lax.rem(z + 16, NZ))

    sib_copies = [remote(acc.at[h, :, 1 - c], sib.at[h], sib_send.at[h], sib_recv.at[h], sibling) for h in range(2)]
    for copy in sib_copies:
        copy.start()

    lane = lax.broadcasted_iota(jnp.int32, (HR, 128), 1)
    row = lax.broadcasted_iota(jnp.int32, (HR, 128), 0)
    for h in range(2):
        k_own = 3 * z + (lane >> 3) - KQ * h
        hit = (row == KQ * (lane & 7) + k_own) & (k_own >= 0) & (k_own < KQ) & (lane < 24)
        pick = jnp.where(hit, 1.0, 0.0).astype(BF16)
        got = jnp.dot(tg[h].reshape(2048, HR), pick, preferred_element_type=F32)
        if h == 0:
            tsel[...] = got
        else:
            tsel[...] += got
    for a in range(NA):
        own = tsel[pl.ds(a, 512, stride=NA), :].astype(BF16)
        part = jnp.zeros((8, 128), F32)
        for d in range(3):
            whole = lax.dot_general(own, left_ref[d], (((0,), (1,)), ((), ())), preferred_element_type=F32)
            part += whole[8 * d:8 * d + 8]
        mixp[:, a] = part

    def ms_copy(q):
        return remote(mixp.at[lax.rem(slab + q, NS)], mslab.at[q - 1], ms_send.at[q - 1], ms_recv.at[q - 1], at_slab(q))

    for q in range(1, NS):
        ms_copy(q).start()

    def x_copy(h, q):
        there = lax.rem(x + q, NX)
        return remote(acc.at[h, there, c], xin.at[q - 1, h], x_send.at[h, q - 1], x_recv.at[h, q - 1], at_x(q))

    for h in range(2):
        sib_copies[h].wait()
        for q in (2, 1, 3):
            there = lax.rem(x + q, NX)
            acc[h, there, c] = acc[h, there, c] + sib[h, there]
            x_copy(h, q).start()

    for q in range(1, NS):
        ms_copy(q).wait_recv()
    total = mixp[slab]
    for q in range(1, NS):
        total += mslab[q - 1]
    mone[...] = total

    def my_copy(q):
        return remote(mone, myin.at[q - 1], my_send.at[q - 1], my_recv.at[q - 1], at_y(q))

    for q in range(1, NY):
        my_copy(q).start()
    for q in range(1, NY):
        my_copy(q).wait_recv()
        total += myin[q - 1]

    def mz_copy(n):
        phase = 0 if n < len(Z_PHASES[0]) else 1
        return remote(mzsend.at[phase], mzin.at[n], mz_send.at[n], mz_recv.at[n], at_z(sum(Z_PHASES, ())[n]))

    def yo_copy(q):
        return remote(red.at[:, :, 128 * q:128 * q + 128], fin.at[y], yo_send.at[q - 1], yo_recv.at[q - 1], at_y(q))

    near, far = range(len(Z_PHASES[0])), range(len(Z_PHASES[0]), len(Z_PHASES[0]) + len(Z_PHASES[1]))
    mzsend[0] = total
    for n in near:
        mz_copy(n).start()
    for n in near:
        mz_copy(n).wait_recv()
        total += mzin[n]
    mzsend[1] = total
    for n in far:
        mz_copy(n).start()

    for h in range(2):
        mine = acc[h, x, c] + sib[h, x]
        for q in range(1, NX):
            x_copy(h, q).wait_recv()
            mine += xin[q - 1, h]
        red[h] = mine
    for q in (2, 1, 3):
        yo_copy(q).start()
    fin[y] = red[:, :, 0:128]

    total = jnp.zeros_like(total)
    for n in far:
        mz_copy(n).wait_recv()
        total += mzin[n]

    lane8 = lax.broadcasted_iota(jnp.int32, (8, 128), 1)
    row8 = lax.broadcasted_iota(jnp.int32, (8, 128), 0)
    put = jnp.where((lane8 & (NA - 1)) == row8, 1.0, 0.0)
    by_l = lax.dot_general(total, put, DOT0, precision=lax.Precision.HIGHEST, preferred_element_type=F32)
    high = by_l.astype(BF16).astype(F32)
    lane32 = lax.broadcasted_iota(jnp.int32, (128, 32, 128), 2)
    row32 = lax.broadcasted_iota(jnp.int32, (128, 32, 128), 1)
    on_diagonal = (lane32 >> 2) == row32
    for n, term in enumerate((high, by_l - high)):
        wide = jnp.where(on_diagonal, jnp.broadcast_to(term[:, None, :], (128, 32, 128)), 0.0)
        spread[:, 128 * n:128 * n + 128] = wide.reshape(4096, 128).astype(BF16)
    both = jnp.dot(rt_hi[...], spread[...], preferred_element_type=F32)
    cycle = both[:, 0:128] + both[:, 128:256]
    cycle += jnp.dot(rt_lo[...], spread[:, 0:128], preferred_element_type=F32)

    for q in range(1, NY):
        remote(
            red.at[:, :, 128 * q:128 * q + 128], fin.at[lax.rem(y + NY - q, NY)],
            yo_send.at[q - 1], yo_recv.at[q - 1], at_y(q),
        ).wait_recv()
    out_ref[...] = fin[...].reshape(O, 128) + cycle

    for q in range(1, NY):
        y_copy(q).wait_send()
        my_copy(q).wait_send()
        yo_copy(q).wait_send()
    for copy in ig_copies:
        copy.wait_send()
    for stream in streams:
        @pl.loop(1, 16)
        def _(step):
            z_copy(stream, step).wait_send()
    for stream in last:
        z_copy(stream, 16).wait_send()
    for h in range(2):
        for q in range(1, NX):
            x_copy(h, q).wait_send()
    for q in range(1, NS):
        ms_copy(q).wait_send()
    for n in range(len(near) + len(far)):
        mz_copy(n).wait_send()


def per_device(amplitudes, ladder_integral, tile_mask, left_factor, right_factor):
    own = amplitudes.reshape(NI * O, 16).T
    integral = ladder_integral.reshape(NY, NZ, 16, 128)
    left = jnp.transpose(left_factor, (1, 0, 2))
    vmem = pl.BlockSpec(memory_space=pltpu.VMEM)
    anywhere = pl.BlockSpec(memory_space=pl.ANY)
    dma = pltpu.SemaphoreType.DMA
    n_mz = sum(len(phase) for phase in Z_PHASES)
    return pl.pallas_call(
        kernel,
        out_shape=jax.ShapeDtypeStruct((O, 128), F32),
        in_specs=[vmem, anywhere, pl.BlockSpec(memory_space=pltpu.SMEM), anywhere, anywhere],
        out_specs=vmem,
        scratch_shapes=[
            pltpu.VMEM((NY, NZ, 16, 128), BF16),
            pltpu.VMEM((3, 128, 512), BF16),
            pltpu.VMEM((128, 32, O), F32),
            pltpu.VMEM((NY, 2, 16, HR), BF16),
            pltpu.VMEM((2, NY, NZ, 16, HR), BF16),
            pltpu.VMEM((NY, NZ, 16, 512), BF16),
            pltpu.VMEM((2, NX, 2, KQ, 512), F32),
            pltpu.VMEM((2, NX, KQ, 512), F32),
            pltpu.VMEM((NX - 1, 2, KQ, 512), F32),
            pltpu.VMEM((2, KQ, 512), F32),
            pltpu.VMEM((NY, 2, KQ, 128), F32),
            pltpu.VMEM((2048, 128), F32),
            pltpu.VMEM((NS, 8, 128), F32),
            pltpu.VMEM((NS - 1, 8, 128), F32),
            pltpu.VMEM((8, 128), F32),
            pltpu.VMEM((NY - 1, 8, 128), F32),
            pltpu.VMEM((2, 8, 128), F32),
            pltpu.VMEM((n_mz, 8, 128), F32),
            pltpu.VMEM((O, 4096), BF16),
            pltpu.VMEM((O, 4096), BF16),
            pltpu.VMEM((4096, 256), BF16),
            dma((3,)),
            pltpu.SemaphoreType.REGULAR,
            dma((NY - 1,)), dma((NY - 1,)),
            dma((4,)), dma((4,)),
            dma((2, 2, 2, 17)), dma((2, 2, 2, 17)),
            dma((2,)), dma((2,)),
            dma((2, NX - 1)), dma((2, NX - 1)),
            dma((NY - 1,)), dma((NY - 1,)),
            dma((NS - 1,)), dma((NS - 1,)),
            dma((NY - 1,)), dma((NY - 1,)),
            dma((n_mz,)), dma((n_mz,)),
        ],
        compiler_params=pltpu.CompilerParams(
            collective_id=0, has_side_effects=True, vmem_limit_bytes=48 * 1024 * 1024
        ),
    )(own, integral, tile_mask.reshape(16), left, right_factor)


def solution(mesh):
    return jax.shard_map(
        per_device,
        mesh=mesh,
        in_specs=(
            P(None, "slab", "pair"),
            P("slab", "pair"),
            P("slab", "pair"),
            P(None, "pair", "slab"),
            P(None, "pair", None),
        ),
        out_specs=P("slab", "pair"),
        check_vma=False,
    )
```

```python
import jax
import jax.numpy as jnp
from jax import lax
from jax.experimental import pallas as pl
from jax.experimental.pallas import tpu as pltpu
from jax.sharding import PartitionSpec as P

O = 384
NA = 4
NI = 8
NY = 4
NZ = 32
NX = 4
NS = 8
KQ = O // NY // 2
HR = NI * KQ
MESH = pl.DeviceIdType.MESH
F32 = jnp.float32
BF16 = jnp.bfloat16
Z_PHASES = ((-3, -2, -1, 1, 2, 3, 4), (-12, -4, 4, 12))
L_PART = 8
DOT0 = (((0,), (0,)), ((), ()))


def kernel(
    t_hbm, int_hbm, mask_ref, left_hbm, right_hbm, out_ref,
    t_ref, int_ref, left_ref, right_ref, tsend, tg, ig, acc, sib, xin, red, fin, rsel, msg, rx, rxf, mixp, mslab, mone, myin, mzsend, mzin,
    rt_hi, rt_lo, spread,
    in_sem, left_in, known, ma_send, ma_recv, ys_send, ys_recv, ig_send, ig_recv, z_send, z_recv, sib_send, sib_recv, x_send, x_recv, yo_send, yo_recv,
    ms_send, ms_recv, my_send, my_recv, mz_send, mz_recv,
):
    pair = lax.axis_index("pair")
    slab = lax.axis_index("slab")
    y, z = lax.div(pair, NZ), lax.rem(pair, NZ)
    x, c = lax.div(slab, 2), lax.rem(slab, 2)

    def at_y(q):
        return {"pair": lax.rem(y + q, NY) * NZ + z, "slab": slab}

    def at_z(q):
        return {"pair": y * NZ + lax.rem(z + q + NZ, NZ), "slab": slab}

    def at_slab(q):
        return {"pair": pair, "slab": lax.rem(slab + q, NS)}

    def at_x(q):
        return {"pair": pair, "slab": lax.rem(x + q, NX) * 2 + c}

    sibling = {"pair": pair, "slab": slab + 1 - 2 * c}

    def remote(src, dst, send, recv, where):
        return pltpu.make_async_remote_copy(
            src_ref=src, dst_ref=dst, send_sem=send, recv_sem=recv, device_id=where, device_id_type=MESH
        )

    loads = [
        pltpu.make_async_copy(here, there, in_sem.at[n])
        for n, (here, there) in enumerate(((t_hbm, t_ref), (int_hbm, int_ref), (left_hbm, left_ref), (right_hbm, right_ref)))
    ]
    for load in loads:
        load.start()

    barrier = pltpu.get_barrier_semaphore()
    senders = [at_y(q) for q in range(1, NY)] + [at_slab(q) for q in range(1, NS)] + [at_z(-1)]
    for where in senders:
        pl.semaphore_signal(barrier, inc=1, device_id=where, device_id_type=MESH)

    loads[0].wait()
    for there in range(NY):
        for h in range(2):
            first = (2 * there + h) * KQ
            tsend[there, h] = jnp.concatenate([t_ref[:, i * O + first:i * O + first + KQ] for i in range(NI)], axis=1)

    pl.semaphore_wait(barrier, len(senders))

    def y_copy(q):
        return remote(tsend.at[lax.rem(y + q, NY)], tg.at[:, y, z], ys_send.at[q - 1], ys_recv.at[q - 1], at_y(q))

    def y_arrived(q):
        return remote(tsend.at[0], tg.at[:, lax.rem(y + NY - q, NY), z], ys_send.at[q - 1], ys_recv.at[q - 1], at_y(q))

    for q in (2, 1, 3):
        y_copy(q).start()
    pl.semaphore_signal(left_in, inc=1, device_id=at_z(1), device_id_type=MESH)
    tg[:, y, z] = tsend[y]

    loads[1].wait()
    for tile in range(16):
        rows = int_ref[tile // 4, (tile % 4) * 8:(tile % 4) * 8 + 8]
        keep = mask_ref[tile].astype(F32)
        ig[tile // 4, (tile % 4) * 8:(tile % 4) * 8 + 8, :, 0:128] = (rows.astype(F32) * keep).astype(BF16)
    acc[...] = jnp.zeros_like(acc)
    mixp[...] = jnp.zeros_like(mixp)

    def ig_copy(n, where):
        slot_src, slot_dst, first, count = ((0, 3, 0, 4), (0, 1, 0, 4), (3, 2, 0, 2), (1, 2, 2, 2))[n]
        return remote(
            ig.at[first:first + count, :, :, slot_src * 128:slot_src * 128 + 128],
            ig.at[first:first + count, :, :, slot_dst * 128:slot_dst * 128 + 128],
            ig_send.at[n], ig_recv.at[n], where,
        )

    ig_copies = [ig_copy(n, at_y(1 if n % 2 == 0 else NY - 1)) for n in range(4)]
    ig_copies[0].start()
    ig_copies[1].start()

    for q in range(1, NY):
        y_arrived(q).wait_recv()

    def z_copy(stream, step, arrived=False):
        way, h, part = stream
        sign = 1 - 2 * way
        slot = lax.rem(z - sign * (step - (0 if arrived else 1)) + NZ, NZ)
        piece = tg.at[h, 2 * part:2 * part + 2, slot]
        return remote(piece, piece, z_send.at[way, h, part, step], z_recv.at[way, h, part, step], at_z(sign))

    streams = [(way, h, part) for h in range(2) for part in range(2) for way in range(2)]
    for stream in streams:
        if stream[0] == 0:
            z_copy(stream, 1).start()
    pl.semaphore_wait(left_in, 1)
    for stream in streams:
        if stream[0] == 1:
            z_copy(stream, 1).start()

    def tell(n):
        for q in (-(1 << n), 1 << n):
            pl.semaphore_signal(known.at[n], inc=1, device_id=at_z(q), device_id_type=MESH)

    def learn(n):
        pl.semaphore_wait(known.at[n], 2)

    tell(0)

    lane = lax.broadcasted_iota(jnp.int32, (HR, 512), 1)
    row = lax.broadcasted_iota(jnp.int32, (HR, 512), 0)
    d_of = (lane >> 3) & 3
    pick = jnp.where((row == KQ * (lane & 7) + 3 * (lane >> 5) + d_of) & (d_of < 3), 1.0, 0.0).astype(BF16)
    got = jnp.dot(tg[:, :, z].reshape(128, HR), pick, preferred_element_type=F32)
    for group in range(4):
        rsel[group] = got[:, 128 * group:128 * group + 128]
    quarter = lax.broadcasted_iota(jnp.int32, (16, 128), 1) >> 5

    @pl.loop(0, 8)
    def _(g):
        h, group = lax.div(g, 4), lax.rem(g, 4)
        own = [rsel[group, pl.ds(pl.multiple_of(h * 64 + there * 16, 16), 16)] for there in range(NY)]
        for zz in range(4):
            put = jnp.zeros((16, 128), F32)
            for there in range(NY):
                shift = (there - zz) % 4 * 32
                moved = pltpu.roll(own[there], shift, 1) if shift else own[there]
                put = jnp.where(quarter == there, moved, put)
            msg[4 * g + zz] = put.astype(BF16)

    rx[z] = msg[z]

    def ma_copy(q):
        return remote(msg.at[lax.rem(z + q, NZ)], rx.at[z], ma_send.at[q - 1], ma_recv.at[q - 1], at_z(q))

    def ma_arrived(q):
        here = rx.at[lax.rem(z + NZ - q, NZ)]
        return remote(here, here, ma_send.at[q - 1], ma_recv.at[q - 1], at_z(q))

    def forward(step):
        for stream in streams:
            z_copy(stream, step, True).wait_recv()
            z_copy(stream, step + 1).start()

    def split(part):
        wide = right_ref[pl.ds(part * L_PART, L_PART)].reshape(L_PART * 32, O).T
        high = wide.astype(BF16)
        where = pl.ds(pl.multiple_of(part * L_PART * 32, L_PART * 32), L_PART * 32)
        rt_hi[:, where] = high
        rt_lo[:, where] = (wide - high.astype(F32)).astype(BF16)

    loads[2].wait()
    loads[3].wait()

    def multiply(first, second):
        rhs = jnp.concatenate([ig[:, first].reshape(64, 512), ig[:, second].reshape(64, 512)], axis=0)
        for h in range(2):
            lhs = jnp.concatenate([tg[h, :, first].reshape(64, HR), tg[h, :, second].reshape(64, HR)], axis=0)
            acc[h] += lax.dot_general(lhs, rhs, DOT0, preferred_element_type=F32).reshape(NX, 2, KQ, 512)

    def unit(distance):
        multiply(lax.rem(z + NZ - distance, NZ), lax.rem(z + distance, NZ))

    def splits(step):
        split(2 * step - 2)
        split(2 * step - 1)

    forward(1)
    learn(0)
    tell(1)
    splits(1)
    forward(2)
    learn(1)
    tell(2)
    splits(2)
    forward(3)
    splits(3)
    ig_copies[0].wait_recv()
    ig_copies[2].start()
    ig_copies[1].wait_recv()
    ig_copies[3].start()
    forward(4)
    learn(2)
    tell(3)
    splits(4)
    forward(5)
    splits(5)

    order = [16 + (1 - 2 * (n % 2)) * ((n + 1) // 2) for n in range(NZ - 1)]
    for step in (6, 7):
        forward(step)
        if step == 6:
            learn(3)
        for q in order[8 * (step - 6):8 * (step - 5)]:
            ma_copy(q).start()
        splits(step)
    split(14)
    split(15)
    ig_copies[2].wait_recv()
    ig_copies[3].wait_recv()

    def units(step):
        unit(2 * step - 15)
        unit(2 * step - 14)

    for step in (8, 9):
        forward(step)
        for q in order[8 * (step - 6):8 * (step - 5)]:
            ma_copy(q).start()
        units(step)

    @pl.loop(10, 12)
    def _(step):
        forward(step)
        units(step)

    forward(12)

    @pl.loop(1, NZ)
    def _(q):
        ma_arrived(q).wait_recv()

    rxf[...] = rx[...].astype(F32).reshape(512, 128)
    blocks = [(d, there) for d in range(3) for there in range(NY)]
    factor = jnp.concatenate([left_ref[d, :, 128 * there:128 * there + 128] for d, there in blocks], axis=0)
    for a in range(NA):
        own = rxf[pl.ds(a, 128, stride=NA), :].astype(BF16)
        whole = lax.dot_general(own, factor, (((0,), (1,)), ((), ())), preferred_element_type=F32)
        part = jnp.zeros((8, 128), F32)
        for n, (d, there) in enumerate(blocks):
            part += whole[32 * there + 8 * d:32 * there + 8 * d + 8, 128 * n:128 * n + 128]
        mixp[:, a] = part

    def ms_copy(q):
        return remote(mixp.at[lax.rem(slab + q, NS)], mslab.at[q - 1], ms_send.at[q - 1], ms_recv.at[q - 1], at_slab(q))

    for q in range(1, NS):
        ms_copy(q).start()
    units(12)
    forward(13)
    units(13)
    forward(14)
    total = mixp[slab]
    for q in range(1, NS):
        ms_copy(q).wait_recv()
        total += mslab[q - 1]
    mone[...] = total

    def my_copy(q):
        return remote(mone, myin.at[q - 1], my_send.at[q - 1], my_recv.at[q - 1], at_y(q))

    for q in (2, 1, 3):
        my_copy(q).start()
    units(14)

    last = [stream for stream in streams if stream[0] == stream[1]]
    for stream in streams:
        z_copy(stream, 15, True).wait_recv()
        if stream in last:
            z_copy(stream, 16).start()

    def mz_copy(n):
        phase = 0 if n < len(Z_PHASES[0]) else 1
        return remote(mzsend.at[phase], mzin.at[n], mz_send.at[n], mz_recv.at[n], at_z(sum(Z_PHASES, ())[n]))

    near, far = range(len(Z_PHASES[0])), range(len(Z_PHASES[0]), len(Z_PHASES[0]) + len(Z_PHASES[1]))
    for q in range(1, NY):
        my_copy(q).wait_recv()
        total += myin[q - 1]
    mzsend[0] = total
    for n in near:
        mz_copy(n).start()
    unit(15)
    for stream in last:
        z_copy(stream, 16, True).wait_recv()
    multiply(z, lax.rem(z + 16, NZ))

    sib_copies = [remote(acc.at[h, :, 1 - c], sib.at[h], sib_send.at[h], sib_recv.at[h], sibling) for h in range(2)]
    for copy in sib_copies:
        copy.start()

    for n in near:
        mz_copy(n).wait_recv()
        total += mzin[n]
    mzsend[1] = total
    for n in far:
        mz_copy(n).start()

    def x_copy(h, q):
        there = lax.rem(x + q, NX)
        return remote(acc.at[h, there, c], xin.at[q - 1, h], x_send.at[h, q - 1], x_recv.at[h, q - 1], at_x(q))

    for h in range(2):
        sib_copies[h].wait()
        for q in (2, 1, 3):
            there = lax.rem(x + q, NX)
            acc[h, there, c] = acc[h, there, c] + sib[h, there]
            x_copy(h, q).start()

    def yo_copy(h, q, src_y):
        return remote(
            red.at[h, :, 128 * q:128 * q + 128], fin.at[src_y, h], yo_send.at[h, q - 1], yo_recv.at[h, q - 1], at_y(q)
        )

    for h in range(2):
        mine = acc[h, x, c] + sib[h, x]
        for q in range(1, NX):
            x_copy(h, q).wait_recv()
            mine += xin[q - 1, h]
        red[h] = mine
        for q in (2, 1, 3):
            yo_copy(h, q, y).start()
        fin[y, h] = mine[:, 0:128]

    total = jnp.zeros_like(total)
    for n in far:
        mz_copy(n).wait_recv()
        total += mzin[n]

    lane8 = lax.broadcasted_iota(jnp.int32, (8, 128), 1)
    row8 = lax.broadcasted_iota(jnp.int32, (8, 128), 0)
    put = jnp.where((lane8 & (NA - 1)) == row8, 1.0, 0.0)
    by_l = lax.dot_general(total, put, DOT0, precision=lax.Precision.HIGHEST, preferred_element_type=F32)
    high = by_l.astype(BF16).astype(F32)
    lane32 = lax.broadcasted_iota(jnp.int32, (128, 32, 128), 2)
    row32 = lax.broadcasted_iota(jnp.int32, (128, 32, 128), 1)
    on_diagonal = (lane32 >> 2) == row32
    for n, term in enumerate((high, by_l - high)):
        wide = jnp.where(on_diagonal, jnp.broadcast_to(term[:, None, :], (128, 32, 128)), 0.0)
        spread[:, 128 * n:128 * n + 128] = wide.reshape(4096, 128).astype(BF16)
    both = jnp.dot(rt_hi[...], spread[...], preferred_element_type=F32)
    cycle = both[:, 0:128] + both[:, 128:256]
    cycle += jnp.dot(rt_lo[...], spread[:, 0:128], preferred_element_type=F32)

    for h in range(2):
        for q in range(1, NY):
            yo_copy(h, q, lax.rem(y + NY - q, NY)).wait_recv()
    out_ref[...] = fin[...].reshape(O, 128) + cycle

    for q in range(1, NY):
        y_copy(q).wait_send()
        my_copy(q).wait_send()
        for h in range(2):
            yo_copy(h, q, y).wait_send()
    for copy in ig_copies:
        copy.wait_send()
    for stream in streams:
        @pl.loop(1, 16)
        def _(step):
            z_copy(stream, step).wait_send()
    for stream in last:
        z_copy(stream, 16).wait_send()
    for h in range(2):
        for q in range(1, NX):
            x_copy(h, q).wait_send()
    for q in range(1, NS):
        ms_copy(q).wait_send()
    for n in range(len(near) + len(far)):
        mz_copy(n).wait_send()

    @pl.loop(1, NZ)
    def _(q):
        ma_copy(q).wait_send()


def per_device(amplitudes, ladder_integral, tile_mask, left_factor, right_factor):
    own = amplitudes.reshape(NI * O, 16).T
    integral = ladder_integral.reshape(NY, NZ, 16, 128)
    left = jnp.transpose(left_factor, (1, 0, 2))
    vmem = pl.BlockSpec(memory_space=pltpu.VMEM)
    hbm = pl.BlockSpec(memory_space=pltpu.HBM)
    dma = pltpu.SemaphoreType.DMA
    n_mz = sum(len(phase) for phase in Z_PHASES)
    return pl.pallas_call(
        kernel,
        out_shape=jax.ShapeDtypeStruct((O, 128), F32),
        in_specs=[hbm, hbm, pl.BlockSpec(memory_space=pltpu.SMEM), hbm, hbm],
        out_specs=vmem,
        scratch_shapes=[
            pltpu.VMEM((16, NI * O), BF16),
            pltpu.VMEM((NY, NZ, 16, 128), BF16),
            pltpu.VMEM((3, 128, 512), BF16),
            pltpu.VMEM((128, 32, O), F32),
            pltpu.VMEM((NY, 2, 16, HR), BF16),
            pltpu.VMEM((2, NY, NZ, 16, HR), BF16),
            pltpu.VMEM((NY, NZ, 16, 512), BF16),
            pltpu.VMEM((2, NX, 2, KQ, 512), F32),
            pltpu.VMEM((2, NX, KQ, 512), F32),
            pltpu.VMEM((NX - 1, 2, KQ, 512), F32),
            pltpu.VMEM((2, KQ, 512), F32),
            pltpu.VMEM((NY, 2, KQ, 128), F32),
            pltpu.VMEM((4, 128, 128), F32),
            pltpu.VMEM((NZ, 16, 128), BF16),
            pltpu.VMEM((NZ, 16, 128), BF16),
            pltpu.VMEM((512, 128), F32),
            pltpu.VMEM((NS, 8, 128), F32),
            pltpu.VMEM((NS - 1, 8, 128), F32),
            pltpu.VMEM((8, 128), F32),
            pltpu.VMEM((NY - 1, 8, 128), F32),
            pltpu.VMEM((2, 8, 128), F32),
            pltpu.VMEM((n_mz, 8, 128), F32),
            pltpu.VMEM((O, 4096), BF16),
            pltpu.VMEM((O, 4096), BF16),
            pltpu.VMEM((4096, 256), BF16),
            dma((4,)),
            pltpu.SemaphoreType.REGULAR,
            pltpu.SemaphoreType.REGULAR((4,)),
            dma((NZ - 1,)), dma((NZ - 1,)),
            dma((NY - 1,)), dma((NY - 1,)),
            dma((4,)), dma((4,)),
            dma((2, 2, 2, 17)), dma((2, 2, 2, 17)),
            dma((2,)), dma((2,)),
            dma((2, NX - 1)), dma((2, NX - 1)),
            dma((2, NY - 1)), dma((2, NY - 1)),
            dma((NS - 1,)), dma((NS - 1,)),
            dma((NY - 1,)), dma((NY - 1,)),
            dma((n_mz,)), dma((n_mz,)),
        ],
        compiler_params=pltpu.CompilerParams(
            collective_id=0, has_side_effects=True, vmem_limit_bytes=60 * 1024 * 1024
        ),
    )(own, integral, tile_mask.reshape(16), left, right_factor)


def solution(mesh):
    return jax.shard_map(
        per_device,
        mesh=mesh,
        in_specs=(
            P(None, "slab", "pair"),
            P("slab", "pair"),
            P("slab", "pair"),
            P(None, "pair", "slab"),
            P(None, "pair", None),
        ),
        out_specs=P("slab", "pair"),
        check_vma=False,
    )
```

```python
import jax
import jax.numpy as jnp
from jax import lax
from jax.experimental import pallas as pl
from jax.experimental.pallas import tpu as pltpu
from jax.sharding import PartitionSpec as P

O = 384
NA = 4
NI = 8
NY = 4
NZ = 32
NX = 4
NS = 8
KQ = O // NY // 2
HR = NI * KQ
MESH = pl.DeviceIdType.MESH
F32 = jnp.float32
BF16 = jnp.bfloat16
Z_PHASES = ((-3, -2, -1, 1, 2, 3, 4), (-12, -4, 4, 12))
L_PART = 8
NEAR = 10
FAR = range(NEAR + 1, NZ - NEAR)
DOT0 = (((0,), (0,)), ((), ()))


def kernel(
    t_hbm, int_hbm, mask_ref, left_hbm, right_hbm, lad_ref, cyc_ref,
    t_ref, int_ref, left_ref, right_ref, tsend, tg, ts, ig, acc, sib, xin, red, fin, rsel, msg, rx, rxf,
    tsel, pick_own, mixp, mixq, mslab, mone, myin, mzsend, mzin, mfin, rt_hi, rt_lo, spread,
    in_sem, left_in, known, ys_send, ys_recv, yt_send, yt_recv, ig_send, ig_recv, z_send, z_recv, l_send, l_recv,
    hand_send, hand_recv, ma_send, ma_recv, sib_send, sib_recv, x_send, x_recv, yo_send, yo_recv,
    ms_send, ms_recv, my_send, my_recv, mz_send, mz_recv, far_send, far_recv,
):
    pair = lax.axis_index("pair")
    slab = lax.axis_index("slab")
    y, z = lax.div(pair, NZ), lax.rem(pair, NZ)
    x, c = lax.div(slab, 2), lax.rem(slab, 2)

    def at_y(q, core=None):
        return {"pair": lax.rem(y + q, NY) * NZ + z, "slab": slab if core is None else 2 * x + core}

    def at_z(q):
        return {"pair": y * NZ + lax.rem(z + q + NZ, NZ), "slab": slab}

    def at_slab(q):
        return {"pair": pair, "slab": lax.rem(slab + q, NS)}

    def at_x(q):
        return {"pair": pair, "slab": lax.rem(x + q, NX) * 2 + c}

    sibling = {"pair": pair, "slab": slab + 1 - 2 * c}

    def remote(src, dst, send, recv, where):
        return pltpu.make_async_remote_copy(
            src_ref=src, dst_ref=dst, send_sem=send, recv_sem=recv, device_id=where, device_id_type=MESH
        )

    loads = [
        pltpu.make_async_copy(here, there, in_sem.at[n])
        for n, (here, there) in enumerate(
            ((t_hbm, t_ref), (int_hbm, int_ref), (left_hbm, left_ref.at[c]), (right_hbm, right_ref))
        )
    ]
    for load in loads:
        load.start()

    rx[...] = jnp.zeros_like(rx)

    barrier = pltpu.get_barrier_semaphore()
    senders = [at_y(q) for q in range(1, NY)] + [at_y(q, 1 - c) for q in range(1, NY)]
    senders += [at_slab(q) for q in range(1, NS)] + [at_z(-1), at_z(-2)]
    for where in senders:
        pl.semaphore_signal(barrier, inc=1, device_id=where, device_id_type=MESH)

    loads[0].wait()
    for there in range(NY):
        for h in range(2):
            first = (2 * there + h) * KQ
            tsend[there, h] = jnp.concatenate([t_ref[:, i * O + first:i * O + first + KQ] for i in range(NI)], axis=1)

    pl.semaphore_wait(barrier, len(senders))

    def y_copy(q):
        return remote(tsend.at[lax.rem(y + q, NY)], tg.at[:, y, z], ys_send.at[q - 1], ys_recv.at[q - 1], at_y(q))

    def y_arrived(q):
        return remote(tsend.at[0], tg.at[:, lax.rem(y + NY - q, NY), z], ys_send.at[q - 1], ys_recv.at[q - 1], at_y(q))

    def yt_copy(q):
        return remote(tsend.at[lax.rem(y + q, NY)], ts.at[:, y, z], yt_send.at[q], yt_recv.at[q], at_y(q, 1))

    def yt_arrived(q):
        return remote(tsend.at[0], ts.at[:, lax.rem(y + NY - q, NY), z], yt_send.at[q], yt_recv.at[q], at_y(q, 1))

    @pl.when(c == 0)
    def _():
        for q in (2, 1, 3, 0):
            yt_copy(q).start()

    for q in (2, 1, 3):
        y_copy(q).start()
    for q in (1, 2):
        pl.semaphore_signal(left_in, inc=1, device_id=at_z(q), device_id_type=MESH)
    tg[:, y, z] = tsend[y]

    def tell(n):
        for q in (-(2 << n), 2 << n):
            pl.semaphore_signal(known.at[n], inc=1, device_id=at_z(q), device_id_type=MESH)

    def learn(n):
        pl.semaphore_wait(known.at[n], 2)

    @pl.when(c == 0)
    def _():
        pl.semaphore_wait(left_in, 2)
        tell(0)

    loads[1].wait()
    for tile in range(16):
        rows = int_ref[tile // 4, (tile % 4) * 8:(tile % 4) * 8 + 8]
        keep = mask_ref[tile].astype(F32)
        ig[tile // 4, (tile % 4) * 8:(tile % 4) * 8 + 8, :, 0:128] = (rows.astype(F32) * keep).astype(BF16)

    def ig_copy(n, where):
        slot_src, slot_dst, first, count = ((0, 3, 0, 4), (0, 1, 0, 4), (3, 2, 0, 2), (1, 2, 2, 2))[n]
        return remote(
            ig.at[first:first + count, :, :, slot_src * 128:slot_src * 128 + 128],
            ig.at[first:first + count, :, :, slot_dst * 128:slot_dst * 128 + 128],
            ig_send.at[n], ig_recv.at[n], where,
        )

    ig_copies = [ig_copy(n, at_y(1 if n % 2 == 0 else NY - 1)) for n in range(4)]
    ig_copies[0].start()
    ig_copies[1].start()

    def ig_forward():
        ig_copies[0].wait_recv()
        ig_copies[2].start()
        ig_copies[1].wait_recv()
        ig_copies[3].start()

    def ig_complete():
        ig_copies[2].wait_recv()
        ig_copies[3].wait_recv()

    def z_copy(stream, step, arrived=False):
        way, of, h = stream
        sign = 1 - 2 * way
        slot = lax.rem(z - sign * (step - (0 if arrived else 1)) + NZ, NZ)
        piece = (ts, tg)[of].at[h, :, slot]
        return remote(piece, piece, z_send.at[way, of, h, step], z_recv.at[way, of, h, step], at_z(sign))

    streams = [(way, of, h) for h in range(2) for of in range(2) for way in range(2)]
    last = [stream for stream in streams if stream[0] == stream[2]]

    def l_copy(way, step):
        slot = lax.rem(z - (1 - 2 * way) * step + NZ, NZ)
        return remote(ts.at[:, :, slot], tg.at[:, :, slot], l_send.at[way, step], l_recv.at[way, step], sibling)

    for q in range(1, NY):
        y_arrived(q).wait_recv()

    @pl.when(c == 1)
    def _():
        for q in range(NY):
            yt_arrived(q).wait_recv()
        for stream in streams:
            if stream[0] == 0:
                z_copy(stream, 1).start()

        pl.semaphore_wait(left_in, 2)
        for stream in streams:
            if stream[0] == 1:
                z_copy(stream, 1).start()

    @pl.when(c == 0)
    def _():
        learn(0)
        tell(1)

    acc[...] = jnp.zeros_like(acc)
    mixp[...] = jnp.zeros_like(mixp)

    lane = lax.broadcasted_iota(jnp.int32, (HR, 512), 1)
    row = lax.broadcasted_iota(jnp.int32, (HR, 512), 0)
    d_of = (lane >> 3) & 3
    pick = jnp.where((row == KQ * (lane & 7) + 3 * (lane >> 5) + d_of) & (d_of < 3), 1.0, 0.0).astype(BF16)
    got = jnp.dot(tg[:, :, z].reshape(128, HR), pick, preferred_element_type=F32)
    for group in range(4):
        rsel[group] = got[:, 128 * group:128 * group + 128]
    quarter = lax.broadcasted_iota(jnp.int32, (16, 128), 1) >> 5

    @pl.loop(0, 8)
    def _(g):
        h, group = lax.div(g, 4), lax.rem(g, 4)
        own = [rsel[group, pl.ds(pl.multiple_of(h * 64 + there * 16, 16), 16)] for there in range(NY)]
        for zz in range(4):
            put = jnp.zeros((16, 128), F32)
            for there in range(NY):
                shift = (there - zz) % 4 * 32
                moved = pltpu.roll(own[there], shift, 1) if shift else own[there]
                put = jnp.where(quarter == there, moved, put)
            msg[4 * g + zz, c] = put.astype(BF16)

    hands = [
        remote(msg.at[:, 1], msg.at[:, 1], hand_send.at[0], hand_recv.at[0], sibling),
        remote(left_ref.at[1], left_ref.at[1], hand_send.at[1], hand_recv.at[1], sibling),
        remote(mixp, mixq, hand_send.at[2], hand_recv.at[2], sibling),
    ]
    loads[2].wait()

    @pl.when(c == 1)
    def _():
        hands[0].start()
        hands[1].start()

    def ma_copy(q):
        return remote(msg.at[lax.rem(z + q, NZ)], rx.at[z], ma_send.at[q - 1], ma_recv.at[q - 1], at_z(q))

    def ma_arrived(q):
        here = rx.at[lax.rem(z + NZ - q, NZ)]
        return remote(here, here, ma_send.at[q - 1], ma_recv.at[q - 1], at_z(q))

    def ms_copy(q):
        there = mixp.at[pl.ds(2 * lax.rem(x + q, NX), 2)]
        return remote(there, mslab.at[q - 1], ms_send.at[q - 1], ms_recv.at[q - 1], at_x(q))

    def my_copy(q):
        return remote(mone, myin.at[q - 1], my_send.at[q - 1], my_recv.at[q - 1], at_y(q))

    def mz_copy(n):
        return remote(mzsend.at[0], mzin.at[n], mz_send.at[n], mz_recv.at[n], at_z(Z_PHASES[0][n]))

    def far_copy(n, of):
        there = {"pair": y * NZ + lax.rem(z + Z_PHASES[1][n] + NZ, NZ), "slab": 2 * x + of}
        return remote(mzsend.at[1, of], mfin.at[n], far_send.at[n, of], far_recv.at[n], there)

    near, far = range(len(Z_PHASES[0])), range(len(Z_PHASES[1]))

    def split(part):
        wide = right_ref[pl.ds(part * L_PART, L_PART)].reshape(L_PART * 32, O).T
        high = wide.astype(BF16)
        where = pl.ds(pl.multiple_of(part * L_PART * 32, L_PART * 32), L_PART * 32)
        rt_hi[:, where] = high
        rt_lo[:, where] = (wide - high.astype(F32)).astype(BF16)

    def multiply(first, second):
        rhs = jnp.concatenate([ig[:, first].reshape(64, 512), ig[:, second].reshape(64, 512)], axis=0)
        for h in range(2):
            lhs = jnp.concatenate([tg[h, :, first].reshape(64, HR), tg[h, :, second].reshape(64, HR)], axis=0)
            acc[h] += lax.dot_general(lhs, rhs, DOT0, preferred_element_type=F32).reshape(NX, 2, KQ, 512)

    def unit(distance):
        multiply(lax.rem(z + NZ - distance, NZ), lax.rem(z + distance, NZ))

    tsel[...] = jnp.zeros_like(tsel)
    lane = lax.broadcasted_iota(jnp.int32, (HR, 128), 1)
    row = lax.broadcasted_iota(jnp.int32, (HR, 128), 0)
    for h in range(2):
        k_own = 3 * z + (lane >> 3) - KQ * h
        hit = (row == KQ * (lane & 7) + k_own) & (k_own >= 0) & (k_own < KQ) & (lane < 24)
        pick_own[h] = jnp.where(hit, 1.0, 0.0).astype(BF16)

    def select(slots):
        got = 0.0
        for h in range(2):
            rows = jnp.concatenate([tg[h, :, slot].reshape(64, HR) for slot in slots], axis=0)
            got += jnp.dot(rows, pick_own[h], preferred_element_type=F32)
        for n, slot in enumerate(slots):
            for there in range(NY):
                first = 64 * n + 16 * there
                tsel[pl.ds(pl.multiple_of((there * NZ + slot) * 16, 16), 16)] = got[first:first + 16]

    def select_at(distance):
        select((lax.rem(z + NZ - distance, NZ), lax.rem(z + distance, NZ)))

    def mix_near():
        for a in range(NA):
            own = tsel[pl.ds(a, 512, stride=NA), :].astype(BF16)
            part = mixp[:, a]
            for d in range(3):
                whole = lax.dot_general(own, left_ref[c, d], (((0,), (1,)), ((), ())), preferred_element_type=F32)
                part += whole[8 * d:8 * d + 8]
            mixp[:, a] = part

    select((z,))
    loads[3].wait()

    @pl.when(c == 1)
    def _():
        def forward(step):
            for stream in streams:
                z_copy(stream, step, True).wait_recv()
                z_copy(stream, step + 1).start()
            for way in range(2):
                l_copy(way, step).start()

        def splits(step):
            split(2 * step - 2)
            split(2 * step - 1)

        @pl.loop(1, 4)
        def _(step):
            forward(step)
            select_at(step)
            splits(step)

        ig_forward()

        @pl.loop(4, 8)
        def _(step):
            forward(step)
            select_at(step)
            splits(step)

        split(14)
        split(15)
        ig_complete()

        def units(step):
            unit(2 * step - 15)
            unit(2 * step - 14)

        @pl.loop(8, NEAR)
        def _(step):
            forward(step)
            select_at(step)
            units(step)

        forward(NEAR)
        select_at(NEAR)
        mix_near()
        hands[2].start()
        units(NEAR)

        @pl.loop(NEAR + 1, 15)
        def _(step):
            forward(step)
            units(step)

        for stream in streams:
            z_copy(stream, 15, True).wait_recv()
            if stream in last:
                z_copy(stream, 16).start()
        for way in range(2):
            l_copy(way, 15).start()
        unit(15)
        for stream in last:
            z_copy(stream, 16, True).wait_recv()
        l_copy(0, 16).start()

    @pl.when(c == 0)
    def _():
        def forward(step):
            for way in range(2):
                l_copy(way, step).wait_recv()

        @pl.loop(0, 9)
        def _(part):
            split(part)

        learn(1)
        tell(2)
        ig_forward()

        @pl.loop(9, 16)
        def _(part):
            split(part)

        hands[0].wait_recv()
        learn(2)

        @pl.loop(0, len(FAR))
        def _(n):
            ma_copy(16 + (1 - 2 * lax.rem(n, 2)) * lax.div(n + 1, 2)).start()

        ig_complete()

        @pl.loop(1, NEAR - 1)
        def _(step):
            forward(step)
            select_at(step)
            unit(step)

        @pl.loop(FAR[0], FAR[-1] + 1)
        def _(q):
            ma_arrived(q).wait_recv()

        hands[1].wait_recv()
        rxf[0] = rx[:, 0].astype(F32).reshape(512, 128)
        rxf[1] = rx[:, 1].astype(F32).reshape(512, 128)
        blocks = [(d, there) for d in range(3) for there in range(NY)]

        @pl.loop(0, 2)
        def _(of):
            factor = jnp.concatenate([left_ref[of, d, :, 128 * there:128 * there + 128] for d, there in blocks], axis=0)
            for a in range(NA):
                own = rxf[of, pl.ds(a, 128, stride=NA), :].astype(BF16)
                whole = lax.dot_general(own, factor, (((0,), (1,)), ((), ())), preferred_element_type=F32)
                part = mixp[:, a]
                for n, (d, there) in enumerate(blocks):
                    part += whole[32 * there + 8 * d:32 * there + 8 * d + 8, 128 * n:128 * n + 128]
                mixp[:, a] = part

        for step in (NEAR - 1, NEAR):
            forward(step)
            select_at(step)
        mix_near()
        hands[2].wait_recv()
        mixp[...] += mixq[...]
        for q in (2, 1, 3):
            ms_copy(q).start()
        total = mixp[pl.ds(2 * x, 2)]
        for q in range(1, NX):
            ms_copy(q).wait_recv()
            total += mslab[q - 1]
        mone[...] = total
        for q in (2, 1, 3):
            my_copy(q).start()
        for q in range(1, NY):
            my_copy(q).wait_recv()
            total += myin[q - 1]
        mzsend[0] = total
        for n in near:
            mz_copy(n).start()
        for n in near:
            mz_copy(n).wait_recv()
            total += mzin[n]
        mzsend[1] = total
        for of in (1, 0):
            for n in far:
                far_copy(n, of).start()

        unit(NEAR - 1)
        unit(NEAR)

        @pl.loop(NEAR + 1, 16)
        def _(step):
            forward(step)
            unit(step)

        l_copy(0, 16).wait_recv()

    multiply(z, lax.rem(z + 16, NZ))

    sib_copies = [remote(acc.at[h, :, 1 - c], sib.at[h], sib_send.at[h], sib_recv.at[h], sibling) for h in range(2)]
    for copy in sib_copies:
        copy.start()

    def x_copy(h, q):
        there = lax.rem(x + q, NX)
        return remote(acc.at[h, there, c], xin.at[q - 1, h], x_send.at[h, q - 1], x_recv.at[h, q - 1], at_x(q))

    for h in range(2):
        sib_copies[h].wait()
        for q in (2, 1, 3):
            there = lax.rem(x + q, NX)
            acc[h, there, c] = acc[h, there, c] + sib[h, there]
            x_copy(h, q).start()

    def yo_copy(h, q, src_y):
        return remote(
            red.at[h, :, 128 * q:128 * q + 128], fin.at[src_y, h], yo_send.at[h, q - 1], yo_recv.at[h, q - 1], at_y(q)
        )

    for h in range(2):
        mine = acc[h, x, c] + sib[h, x]
        for q in range(1, NX):
            x_copy(h, q).wait_recv()
            mine += xin[q - 1, h]
        red[h] = mine
        for q in (2, 1, 3):
            yo_copy(h, q, y).start()
        fin[y, h] = mine[:, 0:128]

    total = jnp.zeros((8, 128), F32)
    for n in far:
        far_copy(n, 0).wait_recv()
        total += mfin[n]

    lane8 = lax.broadcasted_iota(jnp.int32, (8, 128), 1)
    row8 = lax.broadcasted_iota(jnp.int32, (8, 128), 0)
    put = jnp.where((lane8 & (NA - 1)) == row8, 1.0, 0.0)
    by_l = lax.dot_general(total, put, DOT0, precision=lax.Precision.HIGHEST, preferred_element_type=F32)
    high = by_l.astype(BF16).astype(F32)
    lane32 = lax.broadcasted_iota(jnp.int32, (128, 32, 128), 2)
    row32 = lax.broadcasted_iota(jnp.int32, (128, 32, 128), 1)
    on_diagonal = (lane32 >> 2) == row32
    for n, term in enumerate((high, by_l - high)):
        wide = jnp.where(on_diagonal, jnp.broadcast_to(term[:, None, :], (128, 32, 128)), 0.0)
        spread[:, 128 * n:128 * n + 128] = wide.reshape(4096, 128).astype(BF16)
    both = jnp.dot(rt_hi[...], spread[...], preferred_element_type=F32)
    cycle = both[:, 0:128] + both[:, 128:256]
    cyc_ref[...] = cycle + jnp.dot(rt_lo[...], spread[:, 0:128], preferred_element_type=F32)

    for h in range(2):
        for q in range(1, NY):
            yo_copy(h, q, lax.rem(y + NY - q, NY)).wait_recv()
    lad_ref[...] = fin[...].reshape(O, 128)

    for q in range(1, NY):
        y_copy(q).wait_send()
        for h in range(2):
            yo_copy(h, q, y).wait_send()
    for copy in ig_copies:
        copy.wait_send()
    for h in range(2):
        for q in range(1, NX):
            x_copy(h, q).wait_send()

    @pl.when(c == 0)
    def _():
        for q in range(NY):
            yt_copy(q).wait_send()
        for q in range(1, NX):
            ms_copy(q).wait_send()
        for q in range(1, NY):
            my_copy(q).wait_send()
        for n in near:
            mz_copy(n).wait_send()
        for of in range(2):
            for n in far:
                far_copy(n, of).wait_send()

        @pl.loop(FAR[0], FAR[-1] + 1)
        def _(q):
            ma_copy(q).wait_send()

    @pl.when(c == 1)
    def _():
        for hand in hands:
            hand.wait_send()
        for stream in streams:
            @pl.loop(1, 16)
            def _(step):
                z_copy(stream, step).wait_send()
        for stream in last:
            z_copy(stream, 16).wait_send()
        for way in range(2):
            @pl.loop(1, 16)
            def _(step):
                l_copy(way, step).wait_send()
        l_copy(0, 16).wait_send()


def per_device(amplitudes, ladder_integral, tile_mask, left_factor, right_factor):
    own = amplitudes.reshape(NI * O, 16).T
    integral = ladder_integral.reshape(NY, NZ, 16, 128)
    left = jnp.transpose(left_factor, (1, 0, 2))
    vmem = pl.BlockSpec(memory_space=pltpu.VMEM)
    hbm = pl.BlockSpec(memory_space=pltpu.HBM)
    dma = pltpu.SemaphoreType.DMA
    n_near, n_far = (len(phase) for phase in Z_PHASES)
    ladder, cycle = pl.pallas_call(
        kernel,
        out_shape=(jax.ShapeDtypeStruct((O, 128), F32), jax.ShapeDtypeStruct((O, 128), F32)),
        in_specs=[hbm, hbm, pl.BlockSpec(memory_space=pltpu.SMEM), hbm, hbm],
        out_specs=(vmem, vmem),
        scratch_shapes=[
            pltpu.VMEM((16, NI * O), BF16),
            pltpu.VMEM((NY, NZ, 16, 128), BF16),
            pltpu.VMEM((2, 3, 128, 512), BF16),
            pltpu.VMEM((128, 32, O), F32),
            pltpu.VMEM((NY, 2, 16, HR), BF16),
            pltpu.VMEM((2, NY, NZ, 16, HR), BF16),
            pltpu.VMEM((2, NY, NZ, 16, HR), BF16),
            pltpu.VMEM((NY, NZ, 16, 512), BF16),
            pltpu.VMEM((2, NX, 2, KQ, 512), F32),
            pltpu.VMEM((2, NX, KQ, 512), F32),
            pltpu.VMEM((NX - 1, 2, KQ, 512), F32),
            pltpu.VMEM((2, KQ, 512), F32),
            pltpu.VMEM((NY, 2, KQ, 128), F32),
            pltpu.VMEM((4, 128, 128), F32),
            pltpu.VMEM((NZ, 2, 16, 128), BF16),
            pltpu.VMEM((NZ, 2, 16, 128), BF16),
            pltpu.VMEM((2, 512, 128), F32),
            pltpu.VMEM((2048, 128), F32),
            pltpu.VMEM((2, HR, 128), BF16),
            pltpu.VMEM((NS, 8, 128), F32),
            pltpu.VMEM((NS, 8, 128), F32),
            pltpu.VMEM((NX - 1, 2, 8, 128), F32),
            pltpu.VMEM((2, 8, 128), F32),
            pltpu.VMEM((NY - 1, 2, 8, 128), F32),
            pltpu.VMEM((2, 2, 8, 128), F32),
            pltpu.VMEM((n_near, 2, 8, 128), F32),
            pltpu.VMEM((n_far, 8, 128), F32),
            pltpu.VMEM((O, 4096), BF16),
            pltpu.VMEM((O, 4096), BF16),
            pltpu.VMEM((4096, 256), BF16),
            dma((4,)),
            pltpu.SemaphoreType.REGULAR,
            pltpu.SemaphoreType.REGULAR((3,)),
            dma((NY - 1,)), dma((NY - 1,)),
            dma((NY,)), dma((NY,)),
            dma((4,)), dma((4,)),
            dma((2, 2, 2, 17)), dma((2, 2, 2, 17)),
            dma((2, 17)), dma((2, 17)),
            dma((4,)), dma((4,)),
            dma((NZ - 1,)), dma((NZ - 1,)),
            dma((2,)), dma((2,)),
            dma((2, NX - 1)), dma((2, NX - 1)),
            dma((2, NY - 1)), dma((2, NY - 1)),
            dma((NX - 1,)), dma((NX - 1,)),
            dma((NY - 1,)), dma((NY - 1,)),
            dma((n_near,)), dma((n_near,)),
            dma((n_far, 2)), dma((n_far,)),
        ],
        compiler_params=pltpu.CompilerParams(
            collective_id=0, has_side_effects=True, vmem_limit_bytes=60 * 1024 * 1024
        ),
    )(own, integral, tile_mask.reshape(16), left, right_factor)
    return ladder + cycle


def solution(mesh):
    return jax.shard_map(
        per_device,
        mesh=mesh,
        in_specs=(
            P(None, "slab", "pair"),
            P("slab", "pair"),
            P("slab", "pair"),
            P(None, "pair", "slab"),
            P(None, "pair", None),
        ),
        out_specs=P("slab", "pair"),
        check_vma=False,
    )
```

```python
import jax
import jax.numpy as jnp
from jax import lax
from jax.experimental import pallas as pl
from jax.experimental.pallas import tpu as pltpu
from jax.sharding import PartitionSpec as P

O = 384
NA = 4
NI = 8
NY = 4
NZ = 32
NX = 4
NS = 8
KQ = O // NY // 2
HR = NI * KQ
MESH = pl.DeviceIdType.MESH
F32 = jnp.float32
BF16 = jnp.bfloat16
Z_PHASES = ((-3, -2, -1, 1, 2, 3, 4), (-12, -4, 4, 12))
L_PART = 8
NEAR = 10
FAR = range(NEAR + 1, NZ - NEAR)
DOT0 = (((0,), (0,)), ((), ()))


def kernel(
    t_hbm, int_hbm, mask_ref, left_hbm, right_hbm, lad_ref, cyc_ref,
    t_ref, int_ref, left_ref, right_ref, tsend, tg, ts, ig, acc, sib, xin, red, fin, rsel, msg, rx, rxf,
    tsel, pick_own, mixp, mixq, mslab, mone, myin, mzsend, mzin, mfin, rt_hi, rt_lo, spread,
    in_sem, left_in, known, ys_send, ys_recv, yt_send, yt_recv, ig_send, ig_recv, z_send, z_recv, l_send, l_recv,
    hand_send, hand_recv, ma_send, ma_recv, sib_send, sib_recv, x_send, x_recv, yo_send, yo_recv,
    ms_send, ms_recv, my_send, my_recv, mz_send, mz_recv, far_send, far_recv,
):
    pair = lax.axis_index("pair")
    slab = lax.axis_index("slab")
    y, z = lax.div(pair, NZ), lax.rem(pair, NZ)
    x, c = lax.div(slab, 2), lax.rem(slab, 2)

    def at_y(q, core=None):
        return {"pair": lax.rem(y + q, NY) * NZ + z, "slab": slab if core is None else 2 * x + core}

    def at_z(q):
        return {"pair": y * NZ + lax.rem(z + q + NZ, NZ), "slab": slab}

    def at_slab(q):
        return {"pair": pair, "slab": lax.rem(slab + q, NS)}

    def at_x(q):
        return {"pair": pair, "slab": lax.rem(x + q, NX) * 2 + c}

    sibling = {"pair": pair, "slab": slab + 1 - 2 * c}

    def remote(src, dst, send, recv, where):
        return pltpu.make_async_remote_copy(
            src_ref=src, dst_ref=dst, send_sem=send, recv_sem=recv, device_id=where, device_id_type=MESH
        )

    loads = [
        pltpu.make_async_copy(here, there, in_sem.at[n])
        for n, (here, there) in enumerate(
            ((t_hbm, t_ref), (int_hbm, int_ref), (left_hbm, left_ref.at[c]), (right_hbm, right_ref))
        )
    ]
    for load in loads:
        load.start()

    rx[...] = jnp.zeros_like(rx)

    barrier = pltpu.get_barrier_semaphore()
    senders = [at_y(q) for q in range(1, NY)] + [at_y(q, 1 - c) for q in range(1, NY)]
    senders += [at_slab(q) for q in range(1, NS)] + [at_z(-1), at_z(-2)]
    for where in senders:
        pl.semaphore_signal(barrier, inc=1, device_id=where, device_id_type=MESH)

    loads[0].wait()
    for there in range(NY):
        for h in range(2):
            first = (2 * there + h) * KQ
            tsend[there, h] = jnp.concatenate([t_ref[:, i * O + first:i * O + first + KQ] for i in range(NI)], axis=1)

    pl.semaphore_wait(barrier, len(senders))

    def y_copy(q):
        return remote(tsend.at[lax.rem(y + q, NY)], tg.at[:, y, z], ys_send.at[q - 1], ys_recv.at[q - 1], at_y(q))

    def y_arrived(q):
        return remote(tsend.at[0], tg.at[:, lax.rem(y + NY - q, NY), z], ys_send.at[q - 1], ys_recv.at[q - 1], at_y(q))

    def yt_copy(q):
        return remote(tsend.at[lax.rem(y + q, NY)], ts.at[:, y, z], yt_send.at[q], yt_recv.at[q], at_y(q, 1))

    def yt_arrived(q):
        return remote(tsend.at[0], ts.at[:, lax.rem(y + NY - q, NY), z], yt_send.at[q], yt_recv.at[q], at_y(q, 1))

    @pl.when(c == 0)
    def _():
        for q in (2, 1, 3, 0):
            yt_copy(q).start()

    for q in (2, 1, 3):
        y_copy(q).start()
    for q in (1, 2):
        pl.semaphore_signal(left_in, inc=1, device_id=at_z(q), device_id_type=MESH)
    tg[:, y, z] = tsend[y]

    def tell(n):
        for q in (-(2 << n), 2 << n):
            pl.semaphore_signal(known.at[n], inc=1, device_id=at_z(q), device_id_type=MESH)

    def learn(n):
        pl.semaphore_wait(known.at[n], 2)

    @pl.when(c == 0)
    def _():
        pl.semaphore_wait(left_in, 2)
        tell(0)

    loads[1].wait()
    for tile in range(16):
        rows = int_ref[tile // 4, (tile % 4) * 8:(tile % 4) * 8 + 8]
        keep = mask_ref[tile].astype(F32)
        ig[tile // 4, (tile % 4) * 8:(tile % 4) * 8 + 8, :, 0:128] = (rows.astype(F32) * keep).astype(BF16)

    def ig_copy(n, where):
        slot_src, slot_dst, first, count = ((0, 3, 0, 4), (0, 1, 0, 4), (3, 2, 0, 2), (1, 2, 2, 2))[n]
        return remote(
            ig.at[first:first + count, :, :, slot_src * 128:slot_src * 128 + 128],
            ig.at[first:first + count, :, :, slot_dst * 128:slot_dst * 128 + 128],
            ig_send.at[n], ig_recv.at[n], where,
        )

    ig_copies = [ig_copy(n, at_y(1 if n % 2 == 0 else NY - 1)) for n in range(4)]
    ig_copies[0].start()
    ig_copies[1].start()

    def ig_forward():
        ig_copies[0].wait_recv()
        ig_copies[2].start()
        ig_copies[1].wait_recv()
        ig_copies[3].start()

    def ig_complete():
        ig_copies[2].wait_recv()
        ig_copies[3].wait_recv()

    def z_copy(stream, step, arrived=False):
        way, of, h = stream
        sign = 1 - 2 * way
        slot = lax.rem(z - sign * (step - (0 if arrived else 1)) + NZ, NZ)
        piece = (ts, tg)[of].at[h, :, slot]
        return remote(piece, piece, z_send.at[way, of, h, step], z_recv.at[way, of, h, step], at_z(sign))

    streams = [(way, of, h) for of in range(2) for h in range(2) for way in range(2)]
    last = [stream for stream in streams if stream[0] == stream[2]]

    def l_copy(way, step):
        slot = lax.rem(z - (1 - 2 * way) * step + NZ, NZ)
        return remote(ts.at[:, :, slot], tg.at[:, :, slot], l_send.at[way, step], l_recv.at[way, step], sibling)

    for q in range(1, NY):
        y_arrived(q).wait_recv()

    @pl.when(c == 1)
    def _():
        for q in range(NY):
            yt_arrived(q).wait_recv()
        for stream in streams:
            if stream[0] == 0:
                z_copy(stream, 1).start()

        pl.semaphore_wait(left_in, 2)
        for stream in streams:
            if stream[0] == 1:
                z_copy(stream, 1).start()

    @pl.when(c == 0)
    def _():
        learn(0)
        tell(1)

    acc[...] = jnp.zeros_like(acc)
    mixp[...] = jnp.zeros_like(mixp)

    lane = lax.broadcasted_iota(jnp.int32, (HR, 512), 1)
    row = lax.broadcasted_iota(jnp.int32, (HR, 512), 0)
    d_of = (lane >> 3) & 3
    pick = jnp.where((row == KQ * (lane & 7) + 3 * (lane >> 5) + d_of) & (d_of < 3), 1.0, 0.0).astype(BF16)
    got = jnp.dot(tg[:, :, z].reshape(128, HR), pick, preferred_element_type=F32)
    for group in range(4):
        rsel[group] = got[:, 128 * group:128 * group + 128]
    quarter = lax.broadcasted_iota(jnp.int32, (16, 128), 1) >> 5

    @pl.loop(0, 8)
    def _(g):
        h, group = lax.div(g, 4), lax.rem(g, 4)
        own = [rsel[group, pl.ds(pl.multiple_of(h * 64 + there * 16, 16), 16)] for there in range(NY)]
        for zz in range(4):
            put = jnp.zeros((16, 128), F32)
            for there in range(NY):
                shift = (there - zz) % 4 * 32
                moved = pltpu.roll(own[there], shift, 1) if shift else own[there]
                put = jnp.where(quarter == there, moved, put)
            msg[4 * g + zz, c] = put.astype(BF16)

    hands = [
        remote(msg.at[:, 1], msg.at[:, 1], hand_send.at[0], hand_recv.at[0], sibling),
        remote(left_ref.at[1], left_ref.at[1], hand_send.at[1], hand_recv.at[1], sibling),
        remote(mixp, mixq, hand_send.at[2], hand_recv.at[2], sibling),
    ]
    loads[2].wait()

    @pl.when(c == 1)
    def _():
        hands[0].start()
        hands[1].start()

    def ma_copy(q):
        return remote(msg.at[lax.rem(z + q, NZ)], rx.at[z], ma_send.at[q - 1], ma_recv.at[q - 1], at_z(q))

    def ma_arrived(q):
        here = rx.at[lax.rem(z + NZ - q, NZ)]
        return remote(here, here, ma_send.at[q - 1], ma_recv.at[q - 1], at_z(q))

    def ms_copy(q):
        there = mixp.at[pl.ds(2 * lax.rem(x + q, NX), 2)]
        return remote(there, mslab.at[q - 1], ms_send.at[q - 1], ms_recv.at[q - 1], at_x(q))

    def my_copy(q):
        return remote(mone, myin.at[q - 1], my_send.at[q - 1], my_recv.at[q - 1], at_y(q))

    def mz_copy(n):
        return remote(mzsend.at[0], mzin.at[n], mz_send.at[n], mz_recv.at[n], at_z(Z_PHASES[0][n]))

    def far_copy(n, of):
        there = {"pair": y * NZ + lax.rem(z + Z_PHASES[1][n] + NZ, NZ), "slab": 2 * x + of}
        return remote(mzsend.at[1, of], mfin.at[n], far_send.at[n, of], far_recv.at[n], there)

    near, far = range(len(Z_PHASES[0])), range(len(Z_PHASES[1]))

    def split(part):
        wide = right_ref[pl.ds(part * L_PART, L_PART)].reshape(L_PART * 32, O).T
        high = wide.astype(BF16)
        where = pl.ds(pl.multiple_of(part * L_PART * 32, L_PART * 32), L_PART * 32)
        rt_hi[:, where] = high
        rt_lo[:, where] = (wide - high.astype(F32)).astype(BF16)

    def multiply(*slots):
        rhs = jnp.concatenate([ig[:, slot].reshape(64, 512) for slot in slots], axis=0)
        for h in range(2):
            lhs = jnp.concatenate([tg[h, :, slot].reshape(64, HR) for slot in slots], axis=0)
            acc[h] += lax.dot_general(lhs, rhs, DOT0, preferred_element_type=F32).reshape(NX, 2, KQ, 512)

    def pair_at(distance):
        return lax.rem(z + NZ - distance, NZ), lax.rem(z + distance, NZ)

    def unit(distance):
        multiply(*pair_at(distance))

    tsel[...] = jnp.zeros_like(tsel)
    lane = lax.broadcasted_iota(jnp.int32, (HR, 128), 1)
    row = lax.broadcasted_iota(jnp.int32, (HR, 128), 0)
    for h in range(2):
        k_own = 3 * z + (lane >> 3) - KQ * h
        hit = (row == KQ * (lane & 7) + k_own) & (k_own >= 0) & (k_own < KQ) & (lane < 24)
        pick_own[h] = jnp.where(hit, 1.0, 0.0).astype(BF16)

    def select(slots):
        got = 0.0
        for h in range(2):
            rows = jnp.concatenate([tg[h, :, slot].reshape(64, HR) for slot in slots], axis=0)
            got += jnp.dot(rows, pick_own[h], preferred_element_type=F32)
        for n, slot in enumerate(slots):
            for there in range(NY):
                first = 64 * n + 16 * there
                tsel[pl.ds(pl.multiple_of((there * NZ + slot) * 16, 16), 16)] = got[first:first + 16]

    def select_at(distance):
        select((lax.rem(z + NZ - distance, NZ), lax.rem(z + distance, NZ)))

    def mix_near():
        for a in range(NA):
            own = tsel[pl.ds(a, 512, stride=NA), :].astype(BF16)
            part = mixp[:, a]
            for d in range(3):
                whole = lax.dot_general(own, left_ref[c, d], (((0,), (1,)), ((), ())), preferred_element_type=F32)
                part += whole[8 * d:8 * d + 8]
            mixp[:, a] = part

    select((z,))
    loads[3].wait()

    @pl.when(c == 1)
    def _():
        def forward(step):
            for n, stream in enumerate(streams):
                z_copy(stream, step, True).wait_recv()
                z_copy(stream, step + 1).start()
                if n == 3:
                    for way in range(2):
                        l_copy(way, step).start()

        def splits(step):
            split(2 * step - 2)
            split(2 * step - 1)

        @pl.loop(1, 4)
        def _(step):
            forward(step)
            select_at(step)
            splits(step)

        ig_forward()

        @pl.loop(4, 8)
        def _(step):
            forward(step)
            select_at(step)
            splits(step)

        split(14)
        split(15)
        ig_complete()

        def units(step):
            multiply(*pair_at(2 * step - 15), *pair_at(2 * step - 14))

        @pl.loop(8, NEAR)
        def _(step):
            forward(step)
            select_at(step)
            units(step)

        forward(NEAR)
        select_at(NEAR)
        mix_near()
        hands[2].start()
        units(NEAR)

        @pl.loop(NEAR + 1, 15)
        def _(step):
            forward(step)
            units(step)

        for n, stream in enumerate(streams):
            z_copy(stream, 15, True).wait_recv()
            if stream in last:
                z_copy(stream, 16).start()
            if n == 3:
                for way in range(2):
                    l_copy(way, 15).start()
        unit(15)
        for n, stream in enumerate(last):
            z_copy(stream, 16, True).wait_recv()
            if n == 1:
                l_copy(0, 16).start()

    @pl.when(c == 0)
    def _():
        def forward(step):
            for way in range(2):
                l_copy(way, step).wait_recv()

        @pl.loop(0, 9)
        def _(part):
            split(part)

        learn(1)
        tell(2)
        ig_forward()

        @pl.loop(9, 16)
        def _(part):
            split(part)

        hands[0].wait_recv()
        learn(2)

        @pl.loop(0, len(FAR))
        def _(n):
            ma_copy(16 + (1 - 2 * lax.rem(n, 2)) * lax.div(n + 1, 2)).start()

        ig_complete()

        @pl.loop(1, NEAR - 1)
        def _(step):
            forward(step)
            select_at(step)
            unit(step)

        @pl.loop(FAR[0], FAR[-1] + 1)
        def _(q):
            ma_arrived(q).wait_recv()

        hands[1].wait_recv()
        rxf[0] = rx[:, 0].astype(F32).reshape(512, 128)
        rxf[1] = rx[:, 1].astype(F32).reshape(512, 128)
        blocks = [(d, there) for d in range(3) for there in range(NY)]

        @pl.loop(0, 2)
        def _(of):
            factor = jnp.concatenate([left_ref[of, d, :, 128 * there:128 * there + 128] for d, there in blocks], axis=0)
            for a in range(NA):
                own = rxf[of, pl.ds(a, 128, stride=NA), :].astype(BF16)
                whole = lax.dot_general(own, factor, (((0,), (1,)), ((), ())), preferred_element_type=F32)
                part = mixp[:, a]
                for n, (d, there) in enumerate(blocks):
                    part += whole[32 * there + 8 * d:32 * there + 8 * d + 8, 128 * n:128 * n + 128]
                mixp[:, a] = part

        for step in (NEAR - 1, NEAR):
            forward(step)
            select_at(step)
        mix_near()
        hands[2].wait_recv()
        mixp[...] += mixq[...]
        for q in (2, 1, 3):
            ms_copy(q).start()
        total = mixp[pl.ds(2 * x, 2)]
        for q in range(1, NX):
            ms_copy(q).wait_recv()
            total += mslab[q - 1]
        mone[...] = total
        for q in (2, 1, 3):
            my_copy(q).start()
        for q in range(1, NY):
            my_copy(q).wait_recv()
            total += myin[q - 1]
        mzsend[0] = total
        for n in near:
            mz_copy(n).start()
        for n in near:
            mz_copy(n).wait_recv()
            total += mzin[n]
        mzsend[1] = total
        for of in (1, 0):
            for n in far:
                far_copy(n, of).start()

        unit(NEAR - 1)
        unit(NEAR)

        @pl.loop(NEAR + 1, 16)
        def _(step):
            forward(step)
            unit(step)

        l_copy(0, 16).wait_recv()

    multiply(z, lax.rem(z + 16, NZ))

    sib_copies = [remote(acc.at[h, :, 1 - c], sib.at[h], sib_send.at[h], sib_recv.at[h], sibling) for h in range(2)]
    for copy in sib_copies:
        copy.start()

    def x_copy(h, q):
        there = lax.rem(x + q, NX)
        return remote(acc.at[h, there, c], xin.at[q - 1, h], x_send.at[h, q - 1], x_recv.at[h, q - 1], at_x(q))

    for h in range(2):
        sib_copies[h].wait()
        for q in (2, 1, 3):
            there = lax.rem(x + q, NX)
            acc[h, there, c] = acc[h, there, c] + sib[h, there]
            x_copy(h, q).start()

    def yo_copy(h, q, src_y):
        return remote(
            red.at[h, :, 128 * q:128 * q + 128], fin.at[src_y, h], yo_send.at[h, q - 1], yo_recv.at[h, q - 1], at_y(q)
        )

    for h in range(2):
        mine = acc[h, x, c] + sib[h, x]
        for q in range(1, NX):
            x_copy(h, q).wait_recv()
            mine += xin[q - 1, h]
        red[h] = mine
        for q in (2, 1, 3):
            yo_copy(h, q, y).start()
        fin[y, h] = mine[:, 0:128]

    total = jnp.zeros((8, 128), F32)
    for n in far:
        far_copy(n, 0).wait_recv()
        total += mfin[n]

    lane8 = lax.broadcasted_iota(jnp.int32, (8, 128), 1)
    row8 = lax.broadcasted_iota(jnp.int32, (8, 128), 0)
    put = jnp.where((lane8 & (NA - 1)) == row8, 1.0, 0.0)
    by_l = lax.dot_general(total, put, DOT0, precision=lax.Precision.HIGHEST, preferred_element_type=F32)
    high = by_l.astype(BF16).astype(F32)
    lane32 = lax.broadcasted_iota(jnp.int32, (128, 32, 128), 2)
    row32 = lax.broadcasted_iota(jnp.int32, (128, 32, 128), 1)
    on_diagonal = (lane32 >> 2) == row32
    for n, term in enumerate((high, by_l - high)):
        wide = jnp.where(on_diagonal, jnp.broadcast_to(term[:, None, :], (128, 32, 128)), 0.0)
        spread[:, 128 * n:128 * n + 128] = wide.reshape(4096, 128).astype(BF16)
    both = jnp.dot(rt_hi[...], spread[...], preferred_element_type=F32)
    cycle = both[:, 0:128] + both[:, 128:256]
    cyc_ref[...] = cycle + jnp.dot(rt_lo[...], spread[:, 0:128], preferred_element_type=F32)

    for h in range(2):
        for q in range(1, NY):
            yo_copy(h, q, lax.rem(y + NY - q, NY)).wait_recv()
    lad_ref[...] = fin[...].reshape(O, 128)

    for q in range(1, NY):
        y_copy(q).wait_send()
        for h in range(2):
            yo_copy(h, q, y).wait_send()
    for copy in ig_copies:
        copy.wait_send()
    for h in range(2):
        for q in range(1, NX):
            x_copy(h, q).wait_send()

    @pl.when(c == 0)
    def _():
        for q in range(NY):
            yt_copy(q).wait_send()
        for q in range(1, NX):
            ms_copy(q).wait_send()
        for q in range(1, NY):
            my_copy(q).wait_send()
        for n in near:
            mz_copy(n).wait_send()
        for of in range(2):
            for n in far:
                far_copy(n, of).wait_send()

        @pl.loop(FAR[0], FAR[-1] + 1)
        def _(q):
            ma_copy(q).wait_send()

    @pl.when(c == 1)
    def _():
        for hand in hands:
            hand.wait_send()
        for stream in streams:
            @pl.loop(1, 16)
            def _(step):
                z_copy(stream, step).wait_send()
        for stream in last:
            z_copy(stream, 16).wait_send()
        for way in range(2):
            @pl.loop(1, 16)
            def _(step):
                l_copy(way, step).wait_send()
        l_copy(0, 16).wait_send()


def per_device(amplitudes, ladder_integral, tile_mask, left_factor, right_factor):
    own = amplitudes.reshape(NI * O, 16).T
    integral = ladder_integral.reshape(NY, NZ, 16, 128)
    left = jnp.transpose(left_factor, (1, 0, 2))
    vmem = pl.BlockSpec(memory_space=pltpu.VMEM)
    hbm = pl.BlockSpec(memory_space=pltpu.HBM)
    dma = pltpu.SemaphoreType.DMA
    n_near, n_far = (len(phase) for phase in Z_PHASES)
    ladder, cycle = pl.pallas_call(
        kernel,
        out_shape=(jax.ShapeDtypeStruct((O, 128), F32), jax.ShapeDtypeStruct((O, 128), F32)),
        in_specs=[hbm, hbm, pl.BlockSpec(memory_space=pltpu.SMEM), hbm, hbm],
        out_specs=(vmem, vmem),
        scratch_shapes=[
            pltpu.VMEM((16, NI * O), BF16),
            pltpu.VMEM((NY, NZ, 16, 128), BF16),
            pltpu.VMEM((2, 3, 128, 512), BF16),
            pltpu.VMEM((128, 32, O), F32),
            pltpu.VMEM((NY, 2, 16, HR), BF16),
            pltpu.VMEM((2, NY, NZ, 16, HR), BF16),
            pltpu.VMEM((2, NY, NZ, 16, HR), BF16),
            pltpu.VMEM((NY, NZ, 16, 512), BF16),
            pltpu.VMEM((2, NX, 2, KQ, 512), F32),
            pltpu.VMEM((2, NX, KQ, 512), F32),
            pltpu.VMEM((NX - 1, 2, KQ, 512), F32),
            pltpu.VMEM((2, KQ, 512), F32),
            pltpu.VMEM((NY, 2, KQ, 128), F32),
            pltpu.VMEM((4, 128, 128), F32),
            pltpu.VMEM((NZ, 2, 16, 128), BF16),
            pltpu.VMEM((NZ, 2, 16, 128), BF16),
            pltpu.VMEM((2, 512, 128), F32),
            pltpu.VMEM((2048, 128), F32),
            pltpu.VMEM((2, HR, 128), BF16),
            pltpu.VMEM((NS, 8, 128), F32),
            pltpu.VMEM((NS, 8, 128), F32),
            pltpu.VMEM((NX - 1, 2, 8, 128), F32),
            pltpu.VMEM((2, 8, 128), F32),
            pltpu.VMEM((NY - 1, 2, 8, 128), F32),
            pltpu.VMEM((2, 2, 8, 128), F32),
            pltpu.VMEM((n_near, 2, 8, 128), F32),
            pltpu.VMEM((n_far, 8, 128), F32),
            pltpu.VMEM((O, 4096), BF16),
            pltpu.VMEM((O, 4096), BF16),
            pltpu.VMEM((4096, 256), BF16),
            dma((4,)),
            pltpu.SemaphoreType.REGULAR,
            pltpu.SemaphoreType.REGULAR((3,)),
            dma((NY - 1,)), dma((NY - 1,)),
            dma((NY,)), dma((NY,)),
            dma((4,)), dma((4,)),
            dma((2, 2, 2, 17)), dma((2, 2, 2, 17)),
            dma((2, 17)), dma((2, 17)),
            dma((4,)), dma((4,)),
            dma((NZ - 1,)), dma((NZ - 1,)),
            dma((2,)), dma((2,)),
            dma((2, NX - 1)), dma((2, NX - 1)),
            dma((2, NY - 1)), dma((2, NY - 1)),
            dma((NX - 1,)), dma((NX - 1,)),
            dma((NY - 1,)), dma((NY - 1,)),
            dma((n_near,)), dma((n_near,)),
            dma((n_far, 2)), dma((n_far,)),
        ],
        compiler_params=pltpu.CompilerParams(
            collective_id=0, has_side_effects=True, vmem_limit_bytes=60 * 1024 * 1024
        ),
    )(own, integral, tile_mask.reshape(16), left, right_factor)
    return ladder + cycle


def solution(mesh):
    return jax.shard_map(
        per_device,
        mesh=mesh,
        in_specs=(
            P(None, "slab", "pair"),
            P("slab", "pair"),
            P("slab", "pair"),
            P(None, "pair", "slab"),
            P(None, "pair", None),
        ),
        out_specs=P("slab", "pair"),
        check_vma=False,
    )
```
